32 devices in a mesh: member: 2 (over y), space: 16 (over z, x, core).
Axes of the slice: x: 2, y: 2, z: 4, core: 2. Of those that a mesh axis runs over, the one named last changes fastest.
Arguments:
- latent: bfloat16 [4, 1024, 1024], P('member', 'space'), may hold values from -6 to 6
- edge_weight: float32 [3, 8192], P(None, 'space'), may hold values from 0.1 to 1
- neighbours: int32 [3, 8192], P(None, 'space'), may hold values from 0 to 1023, as said below
- band_rows: int32 [16], P('space'), may hold values from 1 to 512, 6144 in all
- w_in: bfloat16 [1024, 1024], replicated, may hold values from -0.1875 to 0.1875
- w_out: bfloat16 [69, 1024], replicated, may hold values from -0.1875 to 0.1875
- target: float32 [69, 8192], P(None, 'space'), may hold values from -80 to 80
Outputs:
- score: float32 [], replicated
- grad_latent: bfloat16 [4, 1024, 1024], P('member', 'space')
- grad_w_out: float32 [69, 1024], P(None, 'space')
The draws below stay inside these ranges and needn't reach their ends.
Inputs may be any that keep to these rules, and one draw needn't show every extreme that they name: `neighbours`: the node of an edge at grid slot g lies in latitude band g // 512 or one of the two bands beside it, node band b holding nodes b * 64 to (b + 1) * 64 - 1. Band b holds real grid points in its first band_rows[b] slots and padding after them; some band is full.
All inputs are finite; a program needn't handle non-finite values. No bound on the sum of `band_rows` on one device may be relied on, other than what follows from the above.
Results may differ from the reference program's by a relative error of at most 0.0075.
Values may be sent and summed in bfloat16 or wider, within the bound.
A program may use at most 64 MiB of HBM per device.

```python
import math
import jax
import jax.numpy as jnp
import numpy as np
from jax import lax

D = 1024
VARS = 69
NEIGH = 3
G_DEV = 512
NODE_DEV = 64
MEMBERS = 4
GRID = 8192
NODES = 1024
N_SPACE = 16


def draw_latent(key, part):
    key = jax.random.fold_in(key, 5)
    common_key, cluster_key, sign_key, noise_key, level_key = jax.random.split(key, 5)
    band_count = NODES // NODE_DEV
    common = jax.random.normal(common_key, (1, NODES, D), jnp.float32)
    noise = jax.random.normal(noise_key, (MEMBERS, NODES, D), jnp.float32)
    cluster = jax.random.normal(cluster_key, (1, NODES, D), jnp.float32)
    order = jax.random.permutation(sign_key, jnp.arange(MEMBERS))
    signs = jnp.where(order < MEMBERS // 2, 1.0, -1.0).astype(jnp.float32)[:, None, None]
    levels = jnp.exp(jax.random.uniform(level_key, (MEMBERS, band_count), jnp.float32, -0.5108, 0.47))
    node_band = jnp.arange(NODES) // NODE_DEV
    halves = jnp.where(jnp.arange(NODES) % NODE_DEV < NODE_DEV // 2, 0.3, 1.0).astype(jnp.float32)
    scales = levels[:, node_band] * halves[None, :]
    values = (common + 0.6 * signs * cluster + 0.35 * noise) * scales[:, :, None]
    return jnp.clip(values, -6.0, 6.0).astype(jnp.bfloat16)


def draw_neighbours(key, part):
    band_key, node_key = jax.random.split(jax.random.fold_in(key, 7))
    band_count = GRID // G_DEV
    column_band = jnp.arange(GRID) // G_DEV
    offset = jax.random.randint(band_key, (NEIGH, GRID), -1, 2)
    owner = jnp.clip(column_band[None, :] + offset, 0, band_count - 1)
    half_nodes = NODE_DEV // 2
    picked = jax.random.randint(node_key, (NEIGH, GRID), 0, half_nodes)
    phase = jnp.where(jnp.arange(GRID) % 4 == 0, 0, half_nodes).astype(jnp.int32)
    within = picked + phase[None, :]
    return (owner * NODE_DEV + within).astype(jnp.int32)


def draw_target(key, part):
    heavy_key, scale_key, value_key = jax.random.split(jax.random.fold_in(key, 11), 3)
    band_count = GRID // G_DEV
    heavy = jax.random.randint(heavy_key, (), 0, band_count)
    base = jnp.exp(jax.random.uniform(scale_key, (band_count,), jnp.float32, -0.6931, 0.4055))
    scales = jnp.where(jnp.arange(band_count) == heavy, 25.0, base)
    values = jnp.clip(jax.random.normal(value_key, (VARS, GRID), jnp.float32), -3.0, 3.0)
    return (values * scales[jnp.arange(GRID) // G_DEV][None, :]).astype(jnp.float32)


def block_levels(own_key, extent, cuts, low, largest):
    def one(position, blocks):
        draws = jax.random.uniform(jax.random.fold_in(jax.random.fold_in(own_key, 6), position), (blocks,), jnp.float32, low / len(cuts), largest / len(cuts))
        return jnp.repeat(jnp.exp(draws), extent[position] // blocks).reshape((-1,) + (1,) * (len(extent) - position - 1))

    gain = one(*cuts[0])
    for cut in cuts[1:]:
        gain = gain * one(*cut)
    return gain


def length_profile(amount, total, limit, lean):
    loads = [(1 << 20) // math.isqrt(rank ** lean) + 1 for rank in range(2, amount + 1)]
    surplus, counts = total - limit - (amount - 1), [1] * (amount - 1)
    while surplus > 0:
        free = [i for i in range(amount - 1) if counts[i] < limit]
        mass, remaining = sum([loads[i] for i in free]), surplus
        for i in free:
            extra = min(limit - counts[i], max(1, remaining * loads[i] // mass), surplus)
            counts[i] = counts[i] + extra
            surplus = surplus - extra
    return np.array([limit] + counts)


def uneven(stream_key, number_of, total, most, skew):
    if number_of == 2:
        one = jax.random.randint(stream_key, (), max(1, total - most), min(most, total - 1) + 1)
        return jnp.stack([one, total - one])
    lengths = jnp.asarray(length_profile(number_of, total, most, skew), jnp.int32)
    couples = (number_of - 1) // 2
    giver, receiver = lengths[1:1 + 2 * couples:2], lengths[2:2 + 2 * couples:2]
    room = jnp.minimum(giver - 1, most - receiver)
    passed = jax.random.randint(jax.random.fold_in(stream_key, 1), (couples,), 0, 1 << 20) % (room + 1)
    lengths = lengths.at[1:1 + 2 * couples:2].set(giver - passed).at[2:2 + 2 * couples:2].set(receiver + passed)
    return lengths[jax.random.permutation(jax.random.fold_in(stream_key, 2), number_of)]


def normal_values(rng, shape, scale, most, held_as=jnp.bfloat16):
    result = scale * jax.random.normal(rng, shape, jnp.float32)
    return jnp.clip(result, min=-most, max=most).astype(held_as)


def setup_inputs(seed: int = 0) -> dict:
    streams_of = jax.random.split(jax.random.key(seed), 8)
    return {
        "latent": draw_latent(jax.random.fold_in(streams_of[7], 71), 0),
        "edge_weight": jnp.clip(jnp.exp(math.log(1.0) - 2.3025851 * jax.random.uniform(streams_of[1], (NEIGH, GRID), jnp.float32) ** block_levels(streams_of[1], (NEIGH, GRID), ((1, 16),), -0.2, 0.2)), 0.1, 1.0),
        "neighbours": draw_neighbours(jax.random.fold_in(streams_of[7], 71), 0),
        "band_rows": uneven(streams_of[3], N_SPACE, N_SPACE * G_DEV * 3 // 4, G_DEV, 1).astype(jnp.int32),
        "w_in": normal_values(streams_of[4], (D, D), D ** -0.5, 0.1875),
        "w_out": normal_values(streams_of[5], (VARS, D), D ** -0.5, 0.1875),
        "target": draw_target(jax.random.fold_in(streams_of[7], 71), 0),
    }


epsilon = 1e-06

def partials(everyone, target_rows, valid_rows):
    deviation = everyone - target_rows[None]
    target_sums = lax.optimization_barrier(jnp.sum(valid_rows * deviation * deviation, axis=(1, 2)))

    def against(member_field):
        spread = everyone - member_field[None]
        return lax.optimization_barrier(jnp.sum(valid_rows * spread * spread, axis=(1, 2)))
    pair_sums = lax.map(against, everyone)
    return (target_sums, pair_sums, jnp.sum(valid_rows))

def finish(target_sums, pair_sums, cell_count, variables):
    members = target_sums.shape[0]
    cells = variables * cell_count
    target_dist = jnp.sqrt(target_sums / cells + epsilon)
    pair_dist = jnp.sqrt(pair_sums / cells + epsilon)
    apart = 1.0 - jnp.eye(members, dtype=jnp.float32)
    pair_coef = apart / pair_dist
    score = jnp.mean(target_dist) - jnp.sum(apart * pair_dist) / (2.0 * members * (members - 1))
    return (score, pair_coef, target_dist)

def member_grads(chosen, everyone, coef_rows, dist_rows, target_rows, valid_rows):
    members = everyone.shape[0]
    others = lax.optimization_barrier(jnp.sum(coef_rows[:, :, None, None] * everyone[None], axis=1))
    spread = lax.optimization_barrier(jnp.sum(coef_rows, axis=1))[:, None, None] * chosen - others
    toward = (chosen - target_rows[None]) / (members * dist_rows[:, None, None])
    return (valid_rows * (toward - spread / (members * (members - 1)))).astype(jnp.bfloat16)

def reference(latent, edge_weight, neighbours, band_rows, w_in, w_out, target):
    members = latent.shape[0]
    grid_count = target.shape[1]
    node_count = latent.shape[1]
    latent_width = latent.shape[2]

    def decode(node_latent):
        picked = jnp.take(node_latent, neighbours, axis=0)
        aggregated = edge_weight[0][:, None] * picked[0].astype(jnp.float32)
        for neighbour in range(1, neighbours.shape[0]):
            aggregated = aggregated + edge_weight[neighbour][:, None] * picked[neighbour].astype(jnp.float32)
        latent_mix = aggregated.astype(jnp.bfloat16)
        preact = jnp.dot(latent_mix, w_in, preferred_element_type=jnp.float32)
        hidden = jax.nn.silu(preact).astype(jnp.bfloat16)
        fields = jnp.dot(w_out, hidden.T, preferred_element_type=jnp.float32).astype(jnp.bfloat16)
        return (fields, preact, hidden)
    fields = lax.map(lambda node_latent: decode(node_latent)[0], latent)
    positions = jnp.arange(grid_count)
    valid_rows = (positions % G_DEV < band_rows[positions // G_DEV]).astype(jnp.float32)
    everyone = fields.astype(jnp.float32)
    target_sums, pair_sums, cell_count = partials(everyone, target, valid_rows)
    score, pair_coef, target_dist = finish(target_sums, pair_sums, cell_count, VARS)

    def one_grad(member_index):
        chosen = everyone[member_index][None]
        return member_grads(chosen, everyone, pair_coef[member_index][None], target_dist[member_index][None], target, valid_rows)[0]
    grad_fields = lax.map(one_grad, jnp.arange(members))
    grid_band = (positions // G_DEV).astype(jnp.int32)
    node_band = (neighbours // NODE_DEV).astype(jnp.int32)
    offset = grid_band[None, :] - node_band
    flat_index = neighbours.reshape(-1)

    def node_sum(grad_mixed, which):
        weights = jnp.where(offset == which, edge_weight, 0.0)
        edge_terms = (weights[:, :, None] * grad_mixed[None]).reshape(-1, latent_width)
        return jax.ops.segment_sum(edge_terms, flat_index, num_segments=node_count)

    def backward(carry, inputs):
        node_latent, grad_member = inputs
        unused, preact, hidden = decode(node_latent)
        carry = carry + jnp.dot(grad_member, hidden, preferred_element_type=jnp.float32)
        back = jnp.dot(grad_member.T, w_out, preferred_element_type=jnp.float32)
        sigmoid_part = jax.nn.sigmoid(preact)
        grad_pre = (back * sigmoid_part * (1.0 + preact * (1.0 - sigmoid_part))).astype(jnp.bfloat16)
        grad_mixed = jnp.dot(grad_pre, w_in.T, preferred_element_type=jnp.float32)
        own = node_sum(grad_mixed, 0)
        from_above = lax.optimization_barrier(node_sum(grad_mixed, 1).astype(jnp.bfloat16)).astype(jnp.float32)
        from_below = lax.optimization_barrier(node_sum(grad_mixed, -1).astype(jnp.bfloat16)).astype(jnp.float32)
        node_grad = own + from_above + from_below
        return (carry, node_grad.astype(jnp.bfloat16))
    start_grad = jnp.zeros((w_out.shape[0], latent_width), jnp.float32)
    grad_w_out, grad_latent = lax.scan(backward, start_grad, (latent, grad_fields))
    return (score, grad_latent, grad_w_out)
```

```python
import functools

import jax
import jax.numpy as jnp
from jax import lax
from jax.experimental import pallas as pl
from jax.experimental.pallas import tpu as pltpu
from jax.sharding import PartitionSpec as P

EPSILON = 1e-06
MESH = pl.DeviceIdType.MESH
F32 = jnp.float32
BF16 = jnp.bfloat16
LANES = 128
STEP = 256


def round_up(value, unit):
    return -(-value // unit) * unit


def dot(a, b, over=((1,), (0,))):
    return lax.dot_general(a, b, (over, ((), ())), preferred_element_type=F32)


def kernel(
    sizes,
    band_rows_ref,
    latent_ref,
    edge_weight_ref,
    neighbours_ref,
    w_in_hbm,
    w_out_ref,
    target_ref,
    score_ref,
    grad_latent_ref,
    grad_w_out_ref,
    w_in,
    w_out,
    nodes_ext,
    spread_hi,
    spread_lo,
    collect_hi,
    collect_lo,
    mixed,
    hidden,
    slope,
    fields_all,
    masked,
    target,
    tiles,
    coefs,
    grad_fields,
    weight_blocks,
    weight_parts,
    weight_sums,
    node_pre,
    node_own,
    rims,
    rims_in,
    load_sem,
    halo_send,
    halo_recv,
    field_send,
    field_recv,
    tile_send,
    tile_recv,
    part_send,
    part_recv,
    sum_send,
    sum_recv,
    rim_send,
    rim_recv,
):
    groups, bands = sizes
    members_dev, nodes, width = latent_ref.shape
    neigh, rows = edge_weight_ref.shape
    variables = w_out_ref.shape[0]
    members = groups * members_dev
    var_rows = fields_all.shape[1]
    blocks = width // LANES
    ranks = bands // blocks
    mine = lax.axis_index("member")
    band = lax.axis_index("space")
    block = band // ranks
    rank = lax.rem(band, ranks)

    barrier = pltpu.get_barrier_semaphore()
    partners = [(mine, lax.rem(band + k, bands)) for k in range(1, bands)]
    for k in range(1, groups):
        for other in range(ranks):
            partners.append((lax.rem(mine + k, groups), block * ranks + other))
    for partner in partners:
        pl.semaphore_signal(barrier, inc=1, device_id=partner, device_id_type=MESH)

    load = pltpu.make_async_copy(w_in_hbm, w_in, load_sem)
    load.start()
    pl.semaphore_wait(barrier, len(partners))

    def remote(src, dst, send, recv, device):
        return pltpu.make_async_remote_copy(
            src_ref=src, dst_ref=dst, send_sem=send, recv_sem=recv, device_id=device, device_id_type=MESH
        )

    halo_up = remote(
        latent_ref, nodes_ext.at[:, pl.ds(0, nodes)], halo_send.at[0], halo_recv.at[0], (mine, band + 1)
    )
    halo_down = remote(
        latent_ref, nodes_ext.at[:, pl.ds(2 * nodes, nodes)], halo_send.at[1], halo_recv.at[1], (mine, band - 1)
    )

    @pl.when(band < bands - 1)
    def _():
        halo_up.start()

    @pl.when(band > 0)
    def _():
        halo_down.start()

    @pl.when(band == 0)
    def _():
        nodes_ext[:, 0:nodes, :] = jnp.zeros((members_dev, nodes, width), BF16)
        rims_in[0] = jnp.zeros(rims_in.shape[1:], BF16)

    @pl.when(band == bands - 1)
    def _():
        nodes_ext[:, 2 * nodes : 3 * nodes, :] = jnp.zeros((members_dev, nodes, width), BF16)
        rims_in[1] = jnp.zeros(rims_in.shape[1:], BF16)

    ext = nodes_ext.shape[1]
    nodes_ext[:, nodes : 2 * nodes, :] = latent_ref[...]
    nodes_ext[:, 3 * nodes :, :] = jnp.zeros((members_dev, ext - 3 * nodes, width), BF16)
    local = neighbours_ref[...] - (band - 1) * nodes
    node_id = lax.broadcasted_iota(jnp.int32, (ext, rows), 0)
    weights = jnp.zeros((ext, rows), F32)
    for k in range(neigh):
        weights = weights + jnp.where(node_id == local[k : k + 1, :], edge_weight_ref[k : k + 1, :], 0.0)
    high = weights.astype(BF16)
    collect_hi[...] = high
    collect_lo[...] = (weights - high.astype(F32)).astype(BF16)
    turned = weights.T
    high = turned.astype(BF16)
    spread_hi[...] = high
    spread_lo[...] = (turned - high.astype(F32)).astype(BF16)

    valid = (lax.broadcasted_iota(jnp.int32, (1, rows), 1) < band_rows_ref[0]).astype(F32)
    target[...] = jnp.zeros(target.shape, F32)
    target[0:variables, :] = target_ref[...] * valid
    w_out[...] = jnp.zeros(w_out.shape, BF16)
    w_out[0:variables, :] = w_out_ref[...]

    @pl.when(band > 0)
    def _():
        halo_up.wait_recv()

    @pl.when(band < bands - 1)
    def _():
        halo_down.wait_recv()

    chunks = width // STEP

    def at(c):
        return pl.ds(pl.multiple_of(c * STEP, STEP), STEP)

    for i in range(members_dev):

        @pl.loop(0, chunks)
        def _(c):
            part = nodes_ext[i, :, at(c)]
            mixed[i * rows : (i + 1) * rows, at(c)] = (
                dot(spread_hi[...], part) + dot(spread_lo[...], part)
            ).astype(BF16)

    load.wait()

    @pl.loop(0, chunks)
    def _(c):
        preact = dot(mixed[...], w_in[:, at(c)])
        sigmoid = 0.5 + 0.5 * jnp.tanh(0.5 * preact)
        hidden[:, at(c)] = (preact * sigmoid).astype(BF16)
        slope[:, at(c)] = sigmoid * (1.0 + preact * (1.0 - sigmoid))

    first = mine * members_dev
    for i in range(members_dev):
        decoded = dot(w_out[0:var_rows, :], hidden[i * rows : (i + 1) * rows, :], ((1,), (1,)))
        fields_all[first + i] = decoded.astype(BF16)
    here = fields_all.at[pl.ds(first, members_dev)]
    field_copies = []
    for k in range(1, groups):
        copy = remote(
            here, here, field_send.at[k - 1], field_recv.at[k - 1], (lax.rem(mine + k, groups), band)
        )
        copy.start()
        field_copies.append(copy)
    for copy in field_copies:
        copy.wait_recv()

    for m in range(members):
        masked[m] = fields_all[m].astype(F32) * valid
    tile_shape = tiles.shape[1:]
    tile_row = lax.broadcasted_iota(jnp.int32, tile_shape, 0)
    tile_lane = lax.broadcasted_iota(jnp.int32, tile_shape, 1)

    def total(array):
        return jnp.sum(jnp.sum(array, axis=0, keepdims=True), axis=1, keepdims=True)

    def distance(a, b):
        gap = a - b
        return total(gap * gap)

    tile = jnp.where(tile_lane == members + 1, total(valid), 0.0)
    if members <= 4:
        for m in range(members):
            place = (tile_row == m) & (tile_lane == members)
            tile = jnp.where(place, distance(masked[m], target[...]), tile)
            for n in range(m):
                place = ((tile_row == m) & (tile_lane == n)) | ((tile_row == n) & (tile_lane == m))
                tile = jnp.where(place, distance(masked[m], masked[n]), tile)
    else:

        def one_member(m, tile):
            own = masked[m]
            here = tile_row == m
            tile = jnp.where(here & (tile_lane == members), distance(own, target[...]), tile)
            return lax.fori_loop(
                0,
                members,
                lambda n, t: jnp.where(here & (tile_lane == n), distance(own, masked[n]), t),
                tile,
            )

        tile = lax.fori_loop(0, members, one_member, tile)
    tiles[band] = tile
    tile_copies = []
    for k in range(1, bands):
        copy = remote(
            tiles.at[band],
            tiles.at[band],
            tile_send.at[k - 1],
            tile_recv.at[k - 1],
            (mine, lax.rem(band + k, bands)),
        )
        copy.start()
        tile_copies.append(copy)
    for copy in tile_copies:
        copy.wait_recv()
    summed = tiles[0]
    for k in range(1, bands):
        summed = summed + tiles[k]

    cells = variables * summed[0:1, members + 1 : members + 2]
    dist = jnp.sqrt(summed / cells + EPSILON)
    in_rows = tile_row < members
    pair = in_rows & (tile_lane < members) & (tile_row != tile_lane)
    own_lane = in_rows & (tile_lane == members)
    score_ref[...] = total(jnp.where(own_lane, dist, 0.0)) / members - total(
        jnp.where(pair, dist, 0.0)
    ) / (2.0 * members * (members - 1))
    inverse = 1.0 / dist
    pair_coef = jnp.where(pair, inverse / (members * (members - 1)), 0.0)
    coef_sum = jnp.sum(pair_coef, axis=1, keepdims=True)
    coefs[...] = jnp.where(
        own_lane, inverse / members, jnp.where(tile_lane == members + 1, coef_sum, pair_coef)
    )
    for i in range(members_dev):
        row = coefs[pl.ds(first + i, 1), :]
        own = masked[first + i]
        others = row[:, 0:1] * masked[0]
        for n in range(1, members):
            others = others + row[:, n : n + 1] * masked[n]
        toward = (own - target[...]) * row[:, members : members + 1]
        grad = toward - (row[:, members + 1 : members + 2] * own - others)
        grad_fields[i, 0:var_rows, :] = grad
        grad_fields[i, var_rows:, :] = jnp.zeros((grad_fields.shape[1] - var_rows, rows), F32)

    var_pad = weight_blocks.shape[1]

    @pl.loop(0, chunks)
    def _(c):
        part = dot(grad_fields[0, 0:var_rows, :].astype(BF16), hidden[0:rows, at(c)])
        for i in range(1, members_dev):
            part = part + dot(
                grad_fields[i, 0:var_rows, :].astype(BF16), hidden[i * rows : (i + 1) * rows, at(c)]
            )
        for j in range(STEP // LANES):
            weight_blocks[c * (STEP // LANES) + j] = part[0:var_pad, j * LANES : (j + 1) * LANES]

    part_copies = []
    for k in range(1, blocks):
        there = lax.rem(block + k, blocks)
        copy = remote(
            weight_blocks.at[there],
            weight_parts.at[block],
            part_send.at[k - 1],
            part_recv.at[k - 1],
            (mine, there * ranks + rank),
        )
        copy.start()
        part_copies.append(copy)
    weight_parts[block] = weight_blocks[block]

    for i in range(members_dev):
        turned_grad = grad_fields[i].T.astype(BF16)

        @pl.loop(0, chunks)
        def _(c):
            back = dot(turned_grad, w_out[:, at(c)])
            grad_pre = (back * slope[i * rows : (i + 1) * rows, at(c)]).astype(BF16)
            gathered = (
                dot(collect_hi[0 : 3 * nodes, :], grad_pre) + dot(collect_lo[0 : 3 * nodes, :], grad_pre)
            ).astype(BF16)
            for side in range(3):
                at_row = (side * members_dev + i) * nodes
                node_pre[at_row : at_row + nodes, at(c)] = gathered[side * nodes : (side + 1) * nodes]

    side_rows = members_dev * nodes

    @pl.loop(0, chunks)
    def _(c):
        grads = dot(node_pre[...], w_in[at(c), :], ((1,), (1,)))
        rims[0, :, at(c)] = grads[0:side_rows].astype(BF16)
        node_own[:, at(c)] = grads[side_rows : 2 * side_rows]
        rims[1, :, at(c)] = grads[2 * side_rows :].astype(BF16)

    rim_down = remote(rims.at[0], rims_in.at[1], rim_send.at[0], rim_recv.at[0], (mine, band - 1))
    rim_up = remote(rims.at[1], rims_in.at[0], rim_send.at[1], rim_recv.at[1], (mine, band + 1))

    @pl.when(band > 0)
    def _():
        rim_down.start()

    @pl.when(band < bands - 1)
    def _():
        rim_up.start()

    for copy in part_copies:
        copy.wait_recv()
    part = weight_parts[0]
    for j in range(1, blocks):
        part = part + weight_parts[j]
    replicas = groups * ranks
    replica = mine * ranks + rank
    weight_sums[replica] = part
    sum_copies = []
    for k in range(1, replicas):
        there = lax.rem(replica + k, replicas)
        copy = remote(
            weight_sums.at[replica],
            weight_sums.at[replica],
            sum_send.at[k - 1],
            sum_recv.at[k - 1],
            (there // ranks, block * ranks + lax.rem(there, ranks)),
        )
        copy.start()
        sum_copies.append(copy)

    @pl.when(band < bands - 1)
    def _():
        rim_down.wait_recv()

    @pl.when(band > 0)
    def _():
        rim_up.wait_recv()

    node_grad = node_own[...] + rims_in[1].astype(F32) + rims_in[0].astype(F32)
    grad_latent_ref[...] = node_grad.astype(BF16).reshape(members_dev, nodes, width)

    for copy in sum_copies:
        copy.wait_recv()
    grad_out = weight_sums[0]
    for k in range(1, replicas):
        grad_out = grad_out + weight_sums[k]
    columns = width // bands
    chosen = grad_out[:, 0:columns]
    for other in range(1, ranks):
        chosen = jnp.where(rank == other, grad_out[:, other * columns : (other + 1) * columns], chosen)
    grad_w_out_ref[...] = chosen[0:variables]

    for copy in field_copies + tile_copies + part_copies + sum_copies:
        copy.wait_send()

    @pl.when(band < bands - 1)
    def _():
        halo_up.wait_send()
        rim_up.wait_send()

    @pl.when(band > 0)
    def _():
        halo_down.wait_send()
        rim_down.wait_send()


def per_device(latent, edge_weight, neighbours, band_rows, w_in, w_out, target):
    groups, bands = lax.axis_size("member"), lax.axis_size("space")
    members_dev, nodes, width = latent.shape
    rows = edge_weight.shape[1]
    variables = w_out.shape[0]
    members = groups * members_dev
    blocks = width // LANES
    replicas = groups * (bands // blocks)
    var_rows = round_up(variables, 16)
    var_pad = round_up(variables, 8)
    ext = round_up(3 * nodes, 256)
    vmem = pl.BlockSpec(memory_space=pltpu.VMEM)
    dma = pltpu.SemaphoreType.DMA
    score, grad_latent, grad_w_out = pl.pallas_call(
        functools.partial(kernel, (groups, bands)),
        out_shape=(
            jax.ShapeDtypeStruct((1, 1), F32),
            jax.ShapeDtypeStruct(latent.shape, BF16),
            jax.ShapeDtypeStruct((variables, width // bands), F32),
        ),
        in_specs=[
            pl.BlockSpec(memory_space=pltpu.SMEM),
            vmem,
            vmem,
            vmem,
            pl.BlockSpec(memory_space=pl.ANY),
            vmem,
            vmem,
        ],
        out_specs=(vmem, vmem, vmem),
        scratch_shapes=[
            pltpu.VMEM((width, width), BF16),
            pltpu.VMEM((LANES, width), BF16),
            pltpu.VMEM((members_dev, ext, width), BF16),
            pltpu.VMEM((rows, ext), BF16),
            pltpu.VMEM((rows, ext), BF16),
            pltpu.VMEM((ext, rows), BF16),
            pltpu.VMEM((ext, rows), BF16),
            pltpu.VMEM((members_dev * rows, width), BF16),
            pltpu.VMEM((members_dev * rows, width), BF16),
            pltpu.VMEM((members_dev * rows, width), F32),
            pltpu.VMEM((members, var_rows, rows), BF16),
            pltpu.VMEM((members, var_rows, rows), F32),
            pltpu.VMEM((var_rows, rows), F32),
            pltpu.VMEM((bands, round_up(members, 8), LANES), F32),
            pltpu.VMEM((round_up(members, 8), LANES), F32),
            pltpu.VMEM((members_dev, LANES, rows), F32),
            pltpu.VMEM((blocks, var_pad, LANES), F32),
            pltpu.VMEM((blocks, var_pad, LANES), F32),
            pltpu.VMEM((replicas, var_pad, LANES), F32),
            pltpu.VMEM((3 * members_dev * nodes, width), BF16),
            pltpu.VMEM((members_dev * nodes, width), F32),
            pltpu.VMEM((2, members_dev * nodes, width), BF16),
            pltpu.VMEM((2, members_dev * nodes, width), BF16),
            dma,
            dma((2,)),
            dma((2,)),
            dma((max(groups - 1, 1),)),
            dma((max(groups - 1, 1),)),
            dma((bands - 1,)),
            dma((bands - 1,)),
            dma((blocks - 1,)),
            dma((blocks - 1,)),
            dma((replicas - 1,)),
            dma((replicas - 1,)),
            dma((2,)),
            dma((2,)),
        ],
        compiler_params=pltpu.CompilerParams(
            collective_id=0, has_side_effects=True, vmem_limit_bytes=50 * 1024 * 1024
        ),
        name="decoder",
    )(band_rows, latent, edge_weight, neighbours, w_in, w_out, target)
    return (score[0, 0], grad_latent, grad_w_out)


def solution(mesh):
    return jax.shard_map(
        per_device,
        mesh=mesh,
        in_specs=(
            P("member", "space", None),
            P(None, "space"),
            P(None, "space"),
            P("space"),
            P(),
            P(),
            P(None, "space"),
        ),
        out_specs=(P(), P("member", "space", None), P(None, "space")),
        check_vma=False,
    )
```

```python
import functools

import jax
import jax.numpy as jnp
from jax import lax
from jax.experimental import pallas as pl
from jax.experimental.pallas import tpu as pltpu
from jax.sharding import PartitionSpec as P

EPSILON = 1e-06
MESH = pl.DeviceIdType.MESH
F32 = jnp.float32
BF16 = jnp.bfloat16
LANES = 128
STEP = 256


def round_up(value, unit):
    return -(-value // unit) * unit


def dot(a, b, over=((1,), (0,))):
    return lax.dot_general(a, b, (over, ((), ())), preferred_element_type=F32)


def kernel(
    sizes,
    latent_ref,
    edge_weight_hbm,
    neighbours_hbm,
    band_rows_hbm,
    w_in_hbm,
    w_out_hbm,
    target_hbm,
    score_ref,
    grad_latent_ref,
    grad_w_out_ref,
    edge_weight_ref,
    neighbours_ref,
    band_rows_ref,
    w_out_ref,
    target_ref,
    w_in,
    w_out,
    nodes_ext,
    spread_hi,
    spread_lo,
    collect_hi,
    collect_lo,
    mixed,
    hidden,
    slope,
    fields_all,
    masked,
    target,
    tiles,
    coefs,
    grad_fields,
    weight_blocks,
    weight_peer,
    weight_half,
    weight_parts,
    weight_sums,
    node_pre,
    node_own,
    rims,
    rims_in,
    load_sem,
    halo_send,
    halo_recv,
    field_send,
    field_recv,
    tile_send,
    tile_recv,
    peer_send,
    peer_recv,
    part_send,
    part_recv,
    sum_send,
    sum_recv,
    rim_send,
    rim_recv,
):
    groups, bands = sizes
    members_dev, nodes, width = latent_ref.shape
    neigh, rows = edge_weight_ref.shape
    variables = w_out_ref.shape[0]
    members = groups * members_dev
    var_rows = fields_all.shape[1]
    blocks = width // LANES
    ranks = bands // blocks
    mine = lax.axis_index("member")
    band = lax.axis_index("space")
    block = band // ranks
    rank = lax.rem(band, ranks)

    barrier = pltpu.get_barrier_semaphore()
    partners = [(mine, lax.rem(band + k, bands)) for k in range(1, bands)]
    for k in range(1, groups):
        for other in range(ranks):
            partners.append((lax.rem(mine + k, groups), block * ranks + other))
    for partner in partners:
        pl.semaphore_signal(barrier, inc=1, device_id=partner, device_id_type=MESH)

    loads = [
        pltpu.make_async_copy(src, dst, load_sem.at[k])
        for k, (src, dst) in enumerate(
            (
                (edge_weight_hbm, edge_weight_ref),
                (neighbours_hbm, neighbours_ref),
                (latent_ref, nodes_ext.at[:, pl.ds(nodes, nodes)]),
                (band_rows_hbm, band_rows_ref),
                (target_hbm, target_ref),
                (w_out_hbm, w_out_ref),
                (w_in_hbm, w_in),
            )
        )
    ]
    for load in loads:
        load.start()
    pl.semaphore_wait(barrier, len(partners))
    chunks = width // STEP

    def remote(src, dst, send, recv, device):
        return pltpu.make_async_remote_copy(
            src_ref=src, dst_ref=dst, send_sem=send, recv_sem=recv, device_id=device, device_id_type=MESH
        )

    halo_up, halo_down = [], []
    for c in range(chunks):
        cut = pl.ds(c * STEP, STEP)
        for way, copies, low in ((0, halo_up, 0), (1, halo_down, 2 * nodes)):
            copies.append(
                remote(
                    latent_ref.at[:, :, cut],
                    nodes_ext.at[:, pl.ds(low, nodes), cut],
                    halo_send.at[way, c],
                    halo_recv.at[way, c],
                    (mine, band + 1 - 2 * way),
                )
            )
    for c in range(chunks):

        @pl.when(band < bands - 1)
        def _():
            halo_up[c].start()

        @pl.when(band > 0)
        def _():
            halo_down[c].start()

    @pl.when(band == 0)
    def _():
        nodes_ext[:, 0:nodes, :] = jnp.zeros((members_dev, nodes, width), BF16)
        rims_in[0] = jnp.zeros(rims_in.shape[1:], BF16)

    @pl.when(band == bands - 1)
    def _():
        nodes_ext[:, 2 * nodes : 3 * nodes, :] = jnp.zeros((members_dev, nodes, width), BF16)
        rims_in[1] = jnp.zeros(rims_in.shape[1:], BF16)

    ext = nodes_ext.shape[1]
    nodes_ext[:, 3 * nodes :, :] = jnp.zeros((members_dev, ext - 3 * nodes, width), BF16)
    loads[0].wait()
    loads[1].wait()
    local = neighbours_ref[...] - (band - 1) * nodes
    node_id = lax.broadcasted_iota(jnp.int32, (ext, rows), 0)
    weights = jnp.zeros((ext, rows), F32)
    for k in range(neigh):
        weights = weights + jnp.where(node_id == local[k : k + 1, :], edge_weight_ref[k : k + 1, :], 0.0)
    high = weights.astype(BF16)
    collect_hi[...] = high
    collect_lo[...] = (weights - high.astype(F32)).astype(BF16)
    turned = weights.T
    high = turned.astype(BF16)
    spread_hi[...] = high
    spread_lo[...] = (turned - high.astype(F32)).astype(BF16)

    for k in range(2, 6):
        loads[k].wait()
    valid = (lax.broadcasted_iota(jnp.int32, (1, rows), 1) < band_rows_ref[0]).astype(F32)
    target[...] = jnp.zeros(target.shape, F32)
    target[0:variables, :] = target_ref[...] * valid
    w_out[...] = jnp.zeros(w_out.shape, BF16)
    w_out[0:variables, :] = w_out_ref[...]

    def at(c):
        return pl.ds(pl.multiple_of(c * STEP, STEP), STEP)

    for c in range(chunks):

        @pl.when(band > 0)
        def _():
            halo_up[c].wait_recv()

        @pl.when(band < bands - 1)
        def _():
            halo_down[c].wait_recv()

        cut = slice(c * STEP, (c + 1) * STEP)
        for i in range(members_dev):
            part = nodes_ext[i, :, cut]
            mixed[i * rows : (i + 1) * rows, cut] = (
                dot(spread_hi[...], part) + dot(spread_lo[...], part)
            ).astype(BF16)

    loads[6].wait()

    @pl.loop(0, chunks)
    def _(c):
        preact = dot(mixed[...], w_in[:, at(c)])
        sigmoid = 0.5 + 0.5 * jnp.tanh(0.5 * preact)
        hidden[:, at(c)] = (preact * sigmoid).astype(BF16)
        slope[:, at(c)] = sigmoid * (1.0 + preact * (1.0 - sigmoid))

    first = mine * members_dev
    for i in range(members_dev):
        decoded = dot(w_out[0:var_rows, :], hidden[i * rows : (i + 1) * rows, :], ((1,), (1,)))
        fields_all[first + i] = decoded.astype(BF16)
    here = fields_all.at[pl.ds(first, members_dev)]
    field_copies = []
    for k in range(1, groups):
        copy = remote(
            here, here, field_send.at[k - 1], field_recv.at[k - 1], (lax.rem(mine + k, groups), band)
        )
        copy.start()
        field_copies.append(copy)
    for copy in field_copies:
        copy.wait_recv()

    for m in range(members):
        masked[m] = fields_all[m].astype(F32) * valid
    tile_shape = tiles.shape[1:]
    tile_row = lax.broadcasted_iota(jnp.int32, tile_shape, 0)
    tile_lane = lax.broadcasted_iota(jnp.int32, tile_shape, 1)

    def total(array):
        return jnp.sum(jnp.sum(array, axis=0, keepdims=True), axis=1, keepdims=True)

    def distance(a, b):
        gap = a - b
        return total(gap * gap)

    tile = jnp.where(tile_lane == members + 1, total(valid), 0.0)
    if members <= 4:
        for m in range(members):
            place = (tile_row == m) & (tile_lane == members)
            tile = jnp.where(place, distance(masked[m], target[...]), tile)
            for n in range(m):
                place = ((tile_row == m) & (tile_lane == n)) | ((tile_row == n) & (tile_lane == m))
                tile = jnp.where(place, distance(masked[m], masked[n]), tile)
    else:

        def one_member(m, tile):
            own = masked[m]
            here = tile_row == m
            tile = jnp.where(here & (tile_lane == members), distance(own, target[...]), tile)
            return lax.fori_loop(
                0,
                members,
                lambda n, t: jnp.where(here & (tile_lane == n), distance(own, masked[n]), t),
                tile,
            )

        tile = lax.fori_loop(0, members, one_member, tile)
    tiles[band] = tile
    tile_copies = []
    for k in range(1, bands):
        copy = remote(
            tiles.at[band],
            tiles.at[band],
            tile_send.at[k - 1],
            tile_recv.at[k - 1],
            (mine, lax.rem(band + k, bands)),
        )
        copy.start()
        tile_copies.append(copy)
    for copy in tile_copies:
        copy.wait_recv()
    summed = tiles[0]
    for k in range(1, bands):
        summed = summed + tiles[k]

    cells = variables * summed[0:1, members + 1 : members + 2]
    dist = jnp.sqrt(summed / cells + EPSILON)
    in_rows = tile_row < members
    pair = in_rows & (tile_lane < members) & (tile_row != tile_lane)
    own_lane = in_rows & (tile_lane == members)
    score_ref[...] = total(jnp.where(own_lane, dist, 0.0)) / members - total(
        jnp.where(pair, dist, 0.0)
    ) / (2.0 * members * (members - 1))
    inverse = 1.0 / dist
    pair_coef = jnp.where(pair, inverse / (members * (members - 1)), 0.0)
    coef_sum = jnp.sum(pair_coef, axis=1, keepdims=True)
    coefs[...] = jnp.where(
        own_lane, inverse / members, jnp.where(tile_lane == members + 1, coef_sum, pair_coef)
    )
    for i in range(members_dev):
        row = coefs[pl.ds(first + i, 1), :]
        own = masked[first + i]
        others = row[:, 0:1] * masked[0]
        for n in range(1, members):
            others = others + row[:, n : n + 1] * masked[n]
        toward = (own - target[...]) * row[:, members : members + 1]
        grad = toward - (row[:, members + 1 : members + 2] * own - others)
        grad_fields[i, 0:var_rows, :] = grad
        grad_fields[i, var_rows:, :] = jnp.zeros((grad_fields.shape[1] - var_rows, rows), F32)

    half_rows = weight_half.shape[1]
    half = lax.rem(rank, 2)

    @pl.loop(0, chunks)
    def _(c):
        part = dot(grad_fields[0, 0:var_rows, :].astype(BF16), hidden[0:rows, at(c)])
        for i in range(1, members_dev):
            part = part + dot(
                grad_fields[i, 0:var_rows, :].astype(BF16), hidden[i * rows : (i + 1) * rows, at(c)]
            )
        for j in range(STEP // LANES):
            for side in range(2):
                weight_blocks[side, c * (STEP // LANES) + j] = part[
                    side * half_rows : (side + 1) * half_rows, j * LANES : (j + 1) * LANES
                ]

    peer_copy = remote(
        weight_blocks.at[1 - half], weight_peer, peer_send, peer_recv, (mine, band + 1 - 2 * half)
    )
    peer_copy.start()
    part_copies = []
    for k in range(1, blocks):
        there = lax.rem(block + k, blocks)
        part_copies.append(
            remote(
                weight_half.at[there],
                weight_parts.at[block],
                part_send.at[k - 1],
                part_recv.at[k - 1],
                (mine, there * ranks + rank),
            )
        )

    for i in range(members_dev):
        turned_grad = grad_fields[i].T.astype(BF16)

        @pl.loop(0, chunks)
        def _(c):
            back = dot(turned_grad, w_out[:, at(c)])
            grad_pre = (back * slope[i * rows : (i + 1) * rows, at(c)]).astype(BF16)
            gathered = (
                dot(collect_hi[0 : 3 * nodes, :], grad_pre) + dot(collect_lo[0 : 3 * nodes, :], grad_pre)
            ).astype(BF16)
            for side in range(3):
                at_row = (side * members_dev + i) * nodes
                node_pre[at_row : at_row + nodes, at(c)] = gathered[side * nodes : (side + 1) * nodes]

        if i == 0:
            peer_copy.wait_recv()
            weight_half[...] = weight_blocks[half] + weight_peer[...]
            for copy in part_copies:
                copy.start()
            weight_parts[block] = weight_half[block]

    side_rows = members_dev * nodes

    rim_down, rim_up = [], []
    for c in range(chunks):
        cut = slice(c * STEP, (c + 1) * STEP)
        grads = dot(node_pre[...], w_in[cut, :], ((1,), (1,)))
        rims[0, c] = grads[0:side_rows].astype(BF16)
        node_own[:, cut] = grads[side_rows : 2 * side_rows]
        rims[1, c] = grads[2 * side_rows :].astype(BF16)
        rim_down.append(
            remote(rims.at[0, c], rims_in.at[1, c], rim_send.at[0, c], rim_recv.at[0, c], (mine, band - 1))
        )
        rim_up.append(
            remote(rims.at[1, c], rims_in.at[0, c], rim_send.at[1, c], rim_recv.at[1, c], (mine, band + 1))
        )

        @pl.when(band > 0)
        def _():
            rim_down[c].start()

        @pl.when(band < bands - 1)
        def _():
            rim_up[c].start()

    for copy in part_copies:
        copy.wait_recv()
    part = weight_parts[0]
    for j in range(1, blocks):
        part = part + weight_parts[j]
    replicas = groups * ranks
    replica = mine * ranks + rank
    weight_sums[replica] = part
    sum_copies = []
    for k in range(1, replicas):
        there = lax.rem(replica + k, replicas)
        copy = remote(
            weight_sums.at[replica],
            weight_sums.at[replica],
            sum_send.at[k - 1],
            sum_recv.at[k - 1],
            (there // ranks, block * ranks + lax.rem(there, ranks)),
        )
        copy.start()
        sum_copies.append(copy)

    for c in range(chunks):

        @pl.when(band < bands - 1)
        def _():
            rim_down[c].wait_recv()

        @pl.when(band > 0)
        def _():
            rim_up[c].wait_recv()

        cut = slice(c * STEP, (c + 1) * STEP)
        node_grad = node_own[:, cut] + rims_in[1, c].astype(F32) + rims_in[0, c].astype(F32)
        grad_latent_ref[:, :, cut] = node_grad.astype(BF16).reshape(members_dev, nodes, STEP)

    for copy in sum_copies:
        copy.wait_recv()
    sides = []
    for side in range(2):
        places = [k for k in range(replicas) if k % ranks % 2 == side]
        side_sum = weight_sums[places[0]]
        for k in places[1:]:
            side_sum = side_sum + weight_sums[k]
        sides.append(side_sum)
    grad_out = jnp.concatenate(sides, axis=0)
    columns = width // bands
    chosen = grad_out[:, 0:columns]
    for other in range(1, ranks):
        chosen = jnp.where(rank == other, grad_out[:, other * columns : (other + 1) * columns], chosen)
    grad_w_out_ref[...] = chosen[0:variables]

    for copy in field_copies + tile_copies + [peer_copy] + part_copies + sum_copies:
        copy.wait_send()
    for c in range(chunks):

        @pl.when(band < bands - 1)
        def _():
            halo_up[c].wait_send()
            rim_up[c].wait_send()

        @pl.when(band > 0)
        def _():
            halo_down[c].wait_send()
            rim_down[c].wait_send()


def per_device(latent, edge_weight, neighbours, band_rows, w_in, w_out, target):
    groups, bands = lax.axis_size("member"), lax.axis_size("space")
    members_dev, nodes, width = latent.shape
    rows = edge_weight.shape[1]
    variables = w_out.shape[0]
    members = groups * members_dev
    blocks = width // LANES
    replicas = groups * (bands // blocks)
    var_rows = round_up(variables, 16)
    chunks = width // STEP
    ext = round_up(3 * nodes, 256)
    vmem = pl.BlockSpec(memory_space=pltpu.VMEM)
    dma = pltpu.SemaphoreType.DMA
    score, grad_latent, grad_w_out = pl.pallas_call(
        functools.partial(kernel, (groups, bands)),
        out_shape=(
            jax.ShapeDtypeStruct((1, 1), F32),
            jax.ShapeDtypeStruct(latent.shape, BF16),
            jax.ShapeDtypeStruct((variables, width // bands), F32),
        ),
        in_specs=[pl.BlockSpec(memory_space=pl.ANY)] * 7,
        out_specs=(vmem, vmem, vmem),
        scratch_shapes=[
            pltpu.VMEM(edge_weight.shape, F32),
            pltpu.VMEM(neighbours.shape, jnp.int32),
            pltpu.SMEM(band_rows.shape, jnp.int32),
            pltpu.VMEM(w_out.shape, BF16),
            pltpu.VMEM(target.shape, F32),
            pltpu.VMEM((width, width), BF16),
            pltpu.VMEM((LANES, width), BF16),
            pltpu.VMEM((members_dev, ext, width), BF16),
            pltpu.VMEM((rows, ext), BF16),
            pltpu.VMEM((rows, ext), BF16),
            pltpu.VMEM((ext, rows), BF16),
            pltpu.VMEM((ext, rows), BF16),
            pltpu.VMEM((members_dev * rows, width), BF16),
            pltpu.VMEM((members_dev * rows, width), BF16),
            pltpu.VMEM((members_dev * rows, width), F32),
            pltpu.VMEM((members, var_rows, rows), BF16),
            pltpu.VMEM((members, var_rows, rows), F32),
            pltpu.VMEM((var_rows, rows), F32),
            pltpu.VMEM((bands, round_up(members, 8), LANES), F32),
            pltpu.VMEM((round_up(members, 8), LANES), F32),
            pltpu.VMEM((members_dev, LANES, rows), F32),
            pltpu.VMEM((2, blocks, var_rows // 2, LANES), F32),
            pltpu.VMEM((blocks, var_rows // 2, LANES), F32),
            pltpu.VMEM((blocks, var_rows // 2, LANES), F32),
            pltpu.VMEM((blocks, var_rows // 2, LANES), F32),
            pltpu.VMEM((replicas, var_rows // 2, LANES), F32),
            pltpu.VMEM((3 * members_dev * nodes, width), BF16),
            pltpu.VMEM((members_dev * nodes, width), F32),
            pltpu.VMEM((2, chunks, members_dev * nodes, STEP), BF16),
            pltpu.VMEM((2, chunks, members_dev * nodes, STEP), BF16),
            dma((7,)),
            dma((2, chunks)),
            dma((2, chunks)),
            dma((max(groups - 1, 1),)),
            dma((max(groups - 1, 1),)),
            dma((bands - 1,)),
            dma((bands - 1,)),
            dma,
            dma,
            dma((blocks - 1,)),
            dma((blocks - 1,)),
            dma((replicas - 1,)),
            dma((replicas - 1,)),
            dma((2, chunks)),
            dma((2, chunks)),
        ],
        compiler_params=pltpu.CompilerParams(
            collective_id=0, has_side_effects=True, vmem_limit_bytes=50 * 1024 * 1024
        ),
        name="decoder",
    )(latent, edge_weight, neighbours, band_rows, w_in, w_out, target)
    return (score[0, 0], grad_latent, grad_w_out)


def solution(mesh):
    return jax.shard_map(
        per_device,
        mesh=mesh,
        in_specs=(
            P("member", "space", None),
            P(None, "space"),
            P(None, "space"),
            P("space"),
            P(),
            P(),
            P(None, "space"),
        ),
        out_specs=(P(), P("member", "space", None), P(None, "space")),
        check_vma=False,
    )
```

```python
import functools

import jax
import jax.numpy as jnp
from jax import lax
from jax.experimental import pallas as pl
from jax.experimental.pallas import tpu as pltpu
from jax.sharding import PartitionSpec as P

EPSILON = 1e-06
MESH = pl.DeviceIdType.MESH
F32 = jnp.float32
BF16 = jnp.bfloat16
LANES = 128
STEP = 256


def round_up(value, unit):
    return -(-value // unit) * unit


def dot(a, b, over=((1,), (0,))):
    return lax.dot_general(a, b, (over, ((), ())), preferred_element_type=F32)


def kernel(
    sizes,
    latent_ref,
    edge_weight_hbm,
    neighbours_hbm,
    band_rows_hbm,
    w_in_hbm,
    w_out_hbm,
    target_hbm,
    score_ref,
    grad_latent_ref,
    grad_w_out_ref,
    edge_weight_ref,
    neighbours_ref,
    band_rows_ref,
    w_out_ref,
    target_ref,
    w_in,
    w_in_turned,
    w_out,
    w_out_turned,
    nodes_ext,
    spread_hi,
    spread_lo,
    collect,
    mixed,
    hidden,
    slope,
    fields_all,
    masked,
    target,
    tiles,
    coefs,
    grad_fields,
    weight_blocks,
    weight_peer,
    weight_half,
    weight_parts,
    weight_sums,
    node_pre,
    node_own,
    rims,
    rims_in,
    load_sem,
    halo_send,
    halo_recv,
    field_send,
    field_recv,
    tile_send,
    tile_recv,
    peer_send,
    peer_recv,
    part_send,
    part_recv,
    sum_send,
    sum_recv,
    rim_send,
    rim_recv,
):
    groups, bands = sizes
    members_dev, nodes, width = latent_ref.shape
    neigh, rows = edge_weight_ref.shape
    variables = w_out_ref.shape[0]
    members = groups * members_dev
    var_rows = fields_all.shape[1]
    blocks = width // LANES
    ranks = bands // blocks
    mine = lax.axis_index("member")
    band = lax.axis_index("space")
    block = band // ranks
    rank = lax.rem(band, ranks)

    barrier = pltpu.get_barrier_semaphore()
    partners = [(mine, lax.rem(band + k, bands)) for k in range(1, bands)]
    for k in range(1, groups):
        for other in range(ranks):
            partners.append((lax.rem(mine + k, groups), block * ranks + other))
    for partner in partners:
        pl.semaphore_signal(barrier, inc=1, device_id=partner, device_id_type=MESH)

    loads = [
        pltpu.make_async_copy(src, dst, load_sem.at[k])
        for k, (src, dst) in enumerate(
            (
                (edge_weight_hbm, edge_weight_ref),
                (neighbours_hbm, neighbours_ref),
                (latent_ref, nodes_ext.at[:, pl.ds(nodes, nodes)]),
                (band_rows_hbm, band_rows_ref),
                (target_hbm, target_ref),
                (w_out_hbm, w_out_ref),
                (w_in_hbm, w_in),
            )
        )
    ]
    for load in loads:
        load.start()
    pl.semaphore_wait(barrier, len(partners))
    chunks = width // STEP

    def remote(src, dst, send, recv, device):
        return pltpu.make_async_remote_copy(
            src_ref=src, dst_ref=dst, send_sem=send, recv_sem=recv, device_id=device, device_id_type=MESH
        )

    halo_up, halo_down = [], []
    for c in range(chunks):
        cut = pl.ds(c * STEP, STEP)
        for way, copies, low in ((0, halo_up, 0), (1, halo_down, 2 * nodes)):
            copies.append(
                remote(
                    latent_ref.at[:, :, cut],
                    nodes_ext.at[:, pl.ds(low, nodes), cut],
                    halo_send.at[way, c],
                    halo_recv.at[way, c],
                    (mine, band + 1 - 2 * way),
                )
            )
    for c in range(chunks):

        @pl.when(band < bands - 1)
        def _():
            halo_up[c].start()

        @pl.when(band > 0)
        def _():
            halo_down[c].start()

    @pl.when(band == 0)
    def _():
        nodes_ext[:, 0:nodes, :] = jnp.zeros((members_dev, nodes, width), BF16)
        rims_in[0] = jnp.zeros(rims_in.shape[1:], BF16)

    @pl.when(band == bands - 1)
    def _():
        nodes_ext[:, 2 * nodes : 3 * nodes, :] = jnp.zeros((members_dev, nodes, width), BF16)
        rims_in[1] = jnp.zeros(rims_in.shape[1:], BF16)

    ext = nodes_ext.shape[1]
    nodes_ext[:, 3 * nodes :, :] = jnp.zeros((members_dev, ext - 3 * nodes, width), BF16)
    loads[0].wait()
    loads[1].wait()
    local = neighbours_ref[...] - (band - 1) * nodes
    node_id = lax.broadcasted_iota(jnp.int32, (ext, rows), 0)
    weights = jnp.zeros((ext, rows), F32)
    for k in range(neigh):
        weights = weights + jnp.where(node_id == local[k : k + 1, :], edge_weight_ref[k : k + 1, :], 0.0)
    high = weights.astype(BF16)
    sides_rows = 3 * nodes
    collect[0:sides_rows, :] = high[0:sides_rows]
    collect[sides_rows:, :] = (weights - high.astype(F32)).astype(BF16)[0:sides_rows]
    turned = weights.T
    high = turned.astype(BF16)
    spread_hi[...] = high
    spread_lo[...] = (turned - high.astype(F32)).astype(BF16)

    for k in range(2, 6):
        loads[k].wait()
    valid = (lax.broadcasted_iota(jnp.int32, (1, rows), 1) < band_rows_ref[0]).astype(F32)
    target[...] = jnp.zeros(target.shape, F32)
    target[0:variables, :] = target_ref[...] * valid
    w_out[...] = jnp.zeros(w_out.shape, BF16)
    w_out[0:variables, :] = w_out_ref[...]
    w_out_turned[...] = w_out[...].astype(F32).T.astype(BF16)

    def at(c):
        return pl.ds(pl.multiple_of(c * STEP, STEP), STEP)

    for c in range(chunks):

        @pl.when(band > 0)
        def _():
            halo_up[c].wait_recv()

        @pl.when(band < bands - 1)
        def _():
            halo_down[c].wait_recv()

        cut = slice(c * STEP, (c + 1) * STEP)
        for i in range(members_dev):
            part = nodes_ext[i, :, cut]
            mixed[i * rows : (i + 1) * rows, cut] = (
                dot(spread_hi[...], part) + dot(spread_lo[...], part)
            ).astype(BF16)

    loads[6].wait()

    @pl.loop(0, chunks)
    def _(c):
        preact = dot(mixed[...], w_in[:, at(c)])
        sigmoid = 0.5 + 0.5 * jnp.tanh(0.5 * preact)
        hidden[:, at(c)] = (preact * sigmoid).astype(BF16)
        slope[:, at(c)] = sigmoid * (1.0 + preact * (1.0 - sigmoid))

    first = mine * members_dev
    field_copies = []
    for i in range(members_dev):
        decoded = dot(hidden[i * rows : (i + 1) * rows, :], w_out_turned[...])
        fields_all[first + i] = decoded.T[0:var_rows].astype(BF16)
        for k in range(1, groups):
            here = fields_all.at[first + i]
            copy = remote(
                here,
                here,
                field_send.at[k - 1, i],
                field_recv.at[k - 1, i],
                (lax.rem(mine + k, groups), band),
            )
            copy.start()
            field_copies.append(copy)

    def turn(c):
        cut = slice(c * STEP, (c + 1) * STEP)
        w_in_turned[:, cut] = w_in[cut, :].T

    for c in range(chunks // 2):
        turn(c)

    tile_shape = tiles.shape[1:]
    tile_row = lax.broadcasted_iota(jnp.int32, tile_shape, 0)
    tile_lane = lax.broadcasted_iota(jnp.int32, tile_shape, 1)

    def total(array):
        return jnp.sum(jnp.sum(array, axis=0, keepdims=True), axis=1, keepdims=True)

    def distance(a, b):
        gap = a - b
        return total(gap * gap)

    tile = jnp.where(tile_lane == members + 1, total(valid), 0.0)
    if members <= 4:
        order = [lax.rem(first + k, members) for k in range(members)]
        for a in range(members):
            if a == members_dev:
                for copy in field_copies:
                    copy.wait_recv()
            m = order[a]
            masked[m] = fields_all[m].astype(F32) * valid
            place = (tile_row == m) & (tile_lane == members)
            tile = jnp.where(place, distance(masked[m], target[...]), tile)
            for n in order[:a]:
                place = ((tile_row == m) & (tile_lane == n)) | ((tile_row == n) & (tile_lane == m))
                tile = jnp.where(place, distance(masked[m], masked[n]), tile)
    else:
        for copy in field_copies:
            copy.wait_recv()
        for m in range(members):
            masked[m] = fields_all[m].astype(F32) * valid

        def one_member(m, tile):
            own = masked[m]
            here = tile_row == m
            tile = jnp.where(here & (tile_lane == members), distance(own, target[...]), tile)
            return lax.fori_loop(
                0,
                members,
                lambda n, t: jnp.where(here & (tile_lane == n), distance(own, masked[n]), t),
                tile,
            )

        tile = lax.fori_loop(0, members, one_member, tile)
    tiles[band] = tile
    tile_copies = []
    for k in range(1, bands):
        copy = remote(
            tiles.at[band],
            tiles.at[band],
            tile_send.at[k - 1],
            tile_recv.at[k - 1],
            (mine, lax.rem(band + k, bands)),
        )
        copy.start()
        tile_copies.append(copy)
    for c in range(chunks // 2, chunks):
        turn(c)
    for copy in tile_copies:
        copy.wait_recv()
    summed = tiles[0]
    for k in range(1, bands):
        summed = summed + tiles[k]

    cells = variables * summed[0:1, members + 1 : members + 2]
    dist = jnp.sqrt(summed / cells + EPSILON)
    in_rows = tile_row < members
    pair = in_rows & (tile_lane < members) & (tile_row != tile_lane)
    own_lane = in_rows & (tile_lane == members)
    score_ref[...] = total(jnp.where(own_lane, dist, 0.0)) / members - total(
        jnp.where(pair, dist, 0.0)
    ) / (2.0 * members * (members - 1))
    inverse = 1.0 / dist
    pair_coef = jnp.where(pair, inverse / (members * (members - 1)), 0.0)
    coef_sum = jnp.sum(pair_coef, axis=1, keepdims=True)
    coefs[...] = jnp.where(
        own_lane, inverse / members, jnp.where(tile_lane == members + 1, coef_sum, pair_coef)
    )
    for i in range(members_dev):
        row = coefs[pl.ds(first + i, 1), :]
        own = masked[first + i]
        others = row[:, 0:1] * masked[0]
        for n in range(1, members):
            others = others + row[:, n : n + 1] * masked[n]
        toward = (own - target[...]) * row[:, members : members + 1]
        grad = toward - (row[:, members + 1 : members + 2] * own - others)
        grad_fields[i, 0:var_rows, :] = grad
        grad_fields[i, var_rows:, :] = jnp.zeros((grad_fields.shape[1] - var_rows, rows), F32)

    half_rows = weight_half.shape[1]
    half = lax.rem(rank, 2)

    @pl.loop(0, chunks)
    def _(c):
        part = dot(grad_fields[0, 0:var_rows, :].astype(BF16), hidden[0:rows, at(c)])
        for i in range(1, members_dev):
            part = part + dot(
                grad_fields[i, 0:var_rows, :].astype(BF16), hidden[i * rows : (i + 1) * rows, at(c)]
            )
        for j in range(STEP // LANES):
            for side in range(2):
                weight_blocks[side, c * (STEP // LANES) + j] = part[
                    side * half_rows : (side + 1) * half_rows, j * LANES : (j + 1) * LANES
                ]

    peer_copy = remote(
        weight_blocks.at[1 - half], weight_peer, peer_send, peer_recv, (mine, band + 1 - 2 * half)
    )
    peer_copy.start()
    part_copies = []
    for k in range(1, blocks):
        there = lax.rem(block + k, blocks)
        part_copies.append(
            remote(
                weight_half.at[there],
                weight_parts.at[block],
                part_send.at[k - 1],
                part_recv.at[k - 1],
                (mine, there * ranks + rank),
            )
        )

    for i in range(members_dev):
        turned_grad = grad_fields[i].T.astype(BF16)

        @pl.loop(0, chunks)
        def _(c):
            back = dot(turned_grad, w_out[:, at(c)])
            grad_pre = (back * slope[i * rows : (i + 1) * rows, at(c)]).astype(BF16)
            terms = dot(collect[...], grad_pre)
            gathered = (terms[0:sides_rows] + terms[sides_rows:]).astype(BF16)
            for side in range(3):
                at_row = (side * members_dev + i) * nodes
                node_pre[at_row : at_row + nodes, at(c)] = gathered[side * nodes : (side + 1) * nodes]

        if i == 0:
            peer_copy.wait_recv()
            weight_half[...] = weight_blocks[half] + weight_peer[...]
            for copy in part_copies:
                copy.start()
            weight_parts[block] = weight_half[block]

    side_rows = members_dev * nodes

    rim_down, rim_up = [], []
    for c in range(chunks):
        cut = slice(c * STEP, (c + 1) * STEP)
        grads = dot(node_pre[...], w_in_turned[:, cut])
        rims[0, c] = grads[0:side_rows].astype(BF16)
        node_own[:, cut] = grads[side_rows : 2 * side_rows]
        rims[1, c] = grads[2 * side_rows :].astype(BF16)
        rim_down.append(
            remote(rims.at[0, c], rims_in.at[1, c], rim_send.at[0, c], rim_recv.at[0, c], (mine, band - 1))
        )
        rim_up.append(
            remote(rims.at[1, c], rims_in.at[0, c], rim_send.at[1, c], rim_recv.at[1, c], (mine, band + 1))
        )

        @pl.when(band > 0)
        def _():
            rim_down[c].start()

        @pl.when(band < bands - 1)
        def _():
            rim_up[c].start()

    for copy in part_copies:
        copy.wait_recv()
    part = weight_parts[0]
    for j in range(1, blocks):
        part = part + weight_parts[j]
    replicas = groups * ranks
    replica = mine * ranks + rank
    weight_sums[replica] = part
    sum_copies = []
    for k in range(1, replicas):
        there = lax.rem(replica + k, replicas)
        copy = remote(
            weight_sums.at[replica],
            weight_sums.at[replica],
            sum_send.at[k - 1],
            sum_recv.at[k - 1],
            (there // ranks, block * ranks + lax.rem(there, ranks)),
        )
        copy.start()
        sum_copies.append(copy)

    for c in range(chunks):

        @pl.when(band < bands - 1)
        def _():
            rim_down[c].wait_recv()

        @pl.when(band > 0)
        def _():
            rim_up[c].wait_recv()

        cut = slice(c * STEP, (c + 1) * STEP)
        node_grad = node_own[:, cut] + rims_in[1, c].astype(F32) + rims_in[0, c].astype(F32)
        grad_latent_ref[:, :, cut] = node_grad.astype(BF16).reshape(members_dev, nodes, STEP)

    for copy in sum_copies:
        copy.wait_recv()
    sides = []
    for side in range(2):
        places = [k for k in range(replicas) if k % ranks % 2 == side]
        side_sum = weight_sums[places[0]]
        for k in places[1:]:
            side_sum = side_sum + weight_sums[k]
        sides.append(side_sum)
    sides.append(jnp.zeros((LANES - 2 * half_rows, LANES), F32))
    grad_out = jnp.concatenate(sides, axis=0).T
    columns = width // bands
    chosen = grad_out[0:columns]
    for other in range(1, ranks):
        chosen = jnp.where(rank == other, grad_out[other * columns : (other + 1) * columns], chosen)
    grad_w_out_ref[...] = chosen[:, 0:variables]

    for copy in field_copies + tile_copies + [peer_copy] + part_copies + sum_copies:
        copy.wait_send()
    for c in range(chunks):

        @pl.when(band < bands - 1)
        def _():
            halo_up[c].wait_send()
            rim_up[c].wait_send()

        @pl.when(band > 0)
        def _():
            halo_down[c].wait_send()
            rim_down[c].wait_send()


def hand_out(score_in, latent_in, weight_in, score_out, latent_out, weight_out, sem):
    copies = [
        pltpu.make_async_copy(latent_in, latent_out, sem.at[0]),
        pltpu.make_async_copy(weight_in, weight_out, sem.at[1]),
    ]
    for copy in copies:
        copy.start()
    score_out[...] = score_in[...]
    for copy in copies:
        copy.wait()


def per_device(latent, edge_weight, neighbours, band_rows, w_in, w_out, target):
    groups, bands = lax.axis_size("member"), lax.axis_size("space")
    members_dev, nodes, width = latent.shape
    rows = edge_weight.shape[1]
    variables = w_out.shape[0]
    members = groups * members_dev
    blocks = width // LANES
    replicas = groups * (bands // blocks)
    var_rows = round_up(variables, 16)
    chunks = width // STEP
    ext = round_up(3 * nodes, 256)
    vmem = pl.BlockSpec(memory_space=pltpu.VMEM)
    dma = pltpu.SemaphoreType.DMA
    score, grad_latent, grad_w_out = pl.pallas_call(
        functools.partial(kernel, (groups, bands)),
        out_shape=(
            jax.ShapeDtypeStruct((1, 1), F32),
            jax.ShapeDtypeStruct(latent.shape, BF16),
            jax.ShapeDtypeStruct((width // bands, variables), F32),
        ),
        in_specs=[pl.BlockSpec(memory_space=pltpu.HBM)] * 7,
        out_specs=(vmem, vmem, vmem),
        scratch_shapes=[
            pltpu.VMEM(edge_weight.shape, F32),
            pltpu.VMEM(neighbours.shape, jnp.int32),
            pltpu.SMEM(band_rows.shape, jnp.int32),
            pltpu.VMEM(w_out.shape, BF16),
            pltpu.VMEM(target.shape, F32),
            pltpu.VMEM((width, width), BF16),
            pltpu.VMEM((width, width), BF16),
            pltpu.VMEM((LANES, width), BF16),
            pltpu.VMEM((width, LANES), BF16),
            pltpu.VMEM((members_dev, ext, width), BF16),
            pltpu.VMEM((rows, ext), BF16),
            pltpu.VMEM((rows, ext), BF16),
            pltpu.VMEM((2 * 3 * nodes, rows), BF16),
            pltpu.VMEM((members_dev * rows, width), BF16),
            pltpu.VMEM((members_dev * rows, width), BF16),
            pltpu.VMEM((members_dev * rows, width), F32),
            pltpu.VMEM((members, var_rows, rows), BF16),
            pltpu.VMEM((members, var_rows, rows), F32),
            pltpu.VMEM((var_rows, rows), F32),
            pltpu.VMEM((bands, members, LANES), F32),
            pltpu.VMEM((members, LANES), F32),
            pltpu.VMEM((members_dev, LANES, rows), F32),
            pltpu.VMEM((2, blocks, var_rows // 2, LANES), F32),
            pltpu.VMEM((blocks, var_rows // 2, LANES), F32),
            pltpu.VMEM((blocks, var_rows // 2, LANES), F32),
            pltpu.VMEM((blocks, var_rows // 2, LANES), F32),
            pltpu.VMEM((replicas, var_rows // 2, LANES), F32),
            pltpu.VMEM((3 * members_dev * nodes, width), BF16),
            pltpu.VMEM((members_dev * nodes, width), F32),
            pltpu.VMEM((2, chunks, members_dev * nodes, STEP), BF16),
            pltpu.VMEM((2, chunks, members_dev * nodes, STEP), BF16),
            dma((7,)),
            dma((2, chunks)),
            dma((2, chunks)),
            dma((max(groups - 1, 1), members_dev)),
            dma((max(groups - 1, 1), members_dev)),
            dma((bands - 1,)),
            dma((bands - 1,)),
            dma,
            dma,
            dma((blocks - 1,)),
            dma((blocks - 1,)),
            dma((replicas - 1,)),
            dma((replicas - 1,)),
            dma((2, chunks)),
            dma((2, chunks)),
        ],
        compiler_params=pltpu.CompilerParams(
            collective_id=0, has_side_effects=True, vmem_limit_bytes=60 * 1024 * 1024
        ),
        name="decoder",
    )(latent, edge_weight, neighbours, band_rows, w_in, w_out, target)
    shapes = (score, grad_latent, grad_w_out)
    score, grad_latent, grad_w_out = pl.pallas_call(
        hand_out,
        out_shape=tuple(jax.ShapeDtypeStruct(a.shape, a.dtype) for a in shapes),
        in_specs=[vmem, pl.BlockSpec(memory_space=pltpu.HBM), pl.BlockSpec(memory_space=pltpu.HBM)],
        out_specs=(vmem, pl.BlockSpec(memory_space=pltpu.HBM), pl.BlockSpec(memory_space=pltpu.HBM)),
        scratch_shapes=[dma((2,))],
        name="hand_out",
    )(score, grad_latent, grad_w_out)
    return (score[0, 0], grad_latent, grad_w_out.T)


def solution(mesh):
    return jax.shard_map(
        per_device,
        mesh=mesh,
        in_specs=(
            P("member", "space", None),
            P(None, "space"),
            P(None, "space"),
            P("space"),
            P(),
            P(),
            P(None, "space"),
        ),
        out_specs=(P(), P("member", "space", None), P(None, "space")),
        check_vma=False,
    )
```

```python
import functools

import jax
import jax.numpy as jnp
from jax import lax
from jax.experimental import pallas as pl
from jax.experimental.pallas import tpu as pltpu
from jax.sharding import PartitionSpec as P

EPSILON = 1e-06
MESH = pl.DeviceIdType.MESH
F32 = jnp.float32
BF16 = jnp.bfloat16
LANES = 128
STEP = 256


def round_up(value, unit):
    return -(-value // unit) * unit


def dot(a, b, over=((1,), (0,))):
    return lax.dot_general(a, b, (over, ((), ())), preferred_element_type=F32)


def kernel(
    sizes,
    latent_ref,
    edge_weight_hbm,
    neighbours_hbm,
    band_rows_hbm,
    w_in_hbm,
    w_out_hbm,
    target_hbm,
    score_ref,
    grad_latent_ref,
    grad_w_out_ref,
    edge_weight_ref,
    neighbours_ref,
    band_rows_ref,
    w_out_ref,
    target_ref,
    w_in,
    w_in_turned,
    w_out,
    w_out_turned,
    nodes_ext,
    spread_hi,
    spread_lo,
    collect,
    mixed,
    hidden,
    slope,
    fields_all,
    masked,
    target,
    tiles,
    coefs,
    grad_fields,
    weight_blocks,
    weight_peer,
    weight_half,
    weight_parts,
    weight_sums,
    node_pre,
    node_own,
    rims,
    rims_in,
    load_sem,
    halo_send,
    halo_recv,
    field_send,
    field_recv,
    tile_send,
    tile_recv,
    peer_send,
    peer_recv,
    part_send,
    part_recv,
    sum_send,
    sum_recv,
    rim_send,
    rim_recv,
):
    groups, bands = sizes
    members_dev, nodes, width = latent_ref.shape
    neigh, rows = edge_weight_ref.shape
    variables = w_out_ref.shape[0]
    members = groups * members_dev
    var_rows = fields_all.shape[1]
    blocks = width // LANES
    ranks = bands // blocks
    mine = lax.axis_index("member")
    band = lax.axis_index("space")
    block = band // ranks
    rank = lax.rem(band, ranks)

    barrier = pltpu.get_barrier_semaphore()
    partners = [(mine, lax.rem(band + k, bands)) for k in range(1, bands)]
    for k in range(1, groups):
        for other in range(ranks):
            partners.append((lax.rem(mine + k, groups), block * ranks + other))
    for partner in partners:
        pl.semaphore_signal(barrier, inc=1, device_id=partner, device_id_type=MESH)

    loads = [
        pltpu.make_async_copy(src, dst, load_sem.at[k])
        for k, (src, dst) in enumerate(
            (
                (edge_weight_hbm, edge_weight_ref),
                (neighbours_hbm, neighbours_ref),
                (latent_ref, nodes_ext.at[:, pl.ds(nodes, nodes)]),
                (band_rows_hbm, band_rows_ref),
                (target_hbm, target_ref),
                (w_out_hbm, w_out_ref),
                (w_in_hbm, w_in),
            )
        )
    ]
    for load in loads:
        load.start()
    pl.semaphore_wait(barrier, len(partners))
    chunks = width // STEP

    def remote(src, dst, send, recv, device):
        return pltpu.make_async_remote_copy(
            src_ref=src, dst_ref=dst, send_sem=send, recv_sem=recv, device_id=device, device_id_type=MESH
        )

    halo_up, halo_down = [], []
    for c in range(chunks):
        cut = pl.ds(c * STEP, STEP)
        for way, copies, low in ((0, halo_up, 0), (1, halo_down, 2 * nodes)):
            copies.append(
                remote(
                    latent_ref.at[:, :, cut],
                    nodes_ext.at[:, pl.ds(low, nodes), cut],
                    halo_send.at[way, c],
                    halo_recv.at[way, c],
                    (mine, band + 1 - 2 * way),
                )
            )
    for c in range(chunks):

        @pl.when(band < bands - 1)
        def _():
            halo_up[c].start()

        @pl.when(band > 0)
        def _():
            halo_down[c].start()

    @pl.when(band == 0)
    def _():
        nodes_ext[:, 0:nodes, :] = jnp.zeros((members_dev, nodes, width), BF16)
        rims_in[0] = jnp.zeros(rims_in.shape[1:], BF16)

    @pl.when(band == bands - 1)
    def _():
        nodes_ext[:, 2 * nodes : 3 * nodes, :] = jnp.zeros((members_dev, nodes, width), BF16)
        rims_in[1] = jnp.zeros(rims_in.shape[1:], BF16)

    ext = nodes_ext.shape[1]
    nodes_ext[:, 3 * nodes :, :] = jnp.zeros((members_dev, ext - 3 * nodes, width), BF16)
    loads[0].wait()
    loads[1].wait()
    local = neighbours_ref[...] - (band - 1) * nodes
    node_id = lax.broadcasted_iota(jnp.int32, (ext, rows), 0)
    weights = jnp.zeros((ext, rows), F32)
    for k in range(neigh):
        weights = weights + jnp.where(node_id == local[k : k + 1, :], edge_weight_ref[k : k + 1, :], 0.0)
    high = weights.astype(BF16)
    sides_rows = 3 * nodes
    collect[0:sides_rows, :] = high[0:sides_rows]
    collect[sides_rows:, :] = (weights - high.astype(F32)).astype(BF16)[0:sides_rows]
    turned = weights.T
    high = turned.astype(BF16)
    spread_hi[...] = high
    spread_lo[...] = (turned - high.astype(F32)).astype(BF16)

    for k in range(2, 6):
        loads[k].wait()
    valid = (lax.broadcasted_iota(jnp.int32, (1, rows), 1) < band_rows_ref[0]).astype(F32)
    target[...] = jnp.zeros(target.shape, F32)
    target[0:variables, :] = target_ref[...] * valid
    w_out[...] = jnp.zeros(w_out.shape, BF16)
    w_out[0:variables, :] = w_out_ref[...]
    w_out_turned[...] = w_out[...].astype(F32).T.astype(BF16)

    def at(c):
        return pl.ds(pl.multiple_of(c * STEP, STEP), STEP)

    first = mine * members_dev
    field_copies = []

    def decode(i, cut):
        of = slice(i * rows, (i + 1) * rows)

        @pl.loop(0, chunks)
        def _(n):
            preact = slope[of, at(n)] + dot(mixed[of], w_in[cut, at(n)])
            sigmoid = 0.5 + 0.5 * jnp.tanh(0.5 * preact)
            hidden[of, at(n)] = (preact * sigmoid).astype(BF16)
            slope[of, at(n)] = sigmoid * (1.0 + preact * (1.0 - sigmoid))

        decoded = dot(hidden[of, :], w_out_turned[...])
        fields_all[first + i] = decoded.T[0:var_rows].astype(BF16)
        for k in range(1, groups):
            here = fields_all.at[first + i]
            copy = remote(
                here,
                here,
                field_send.at[k - 1, i],
                field_recv.at[k - 1, i],
                (lax.rem(mine + k, groups), band),
            )
            copy.start()
            field_copies.append(copy)

    for c in range(chunks):

        @pl.when(band > 0)
        def _():
            halo_up[c].wait_recv()

        @pl.when(band < bands - 1)
        def _():
            halo_down[c].wait_recv()

        if c == 0:
            loads[6].wait()
        cut = slice(c * STEP, (c + 1) * STEP)
        for i in range(members_dev):
            of = slice(i * rows, (i + 1) * rows)
            part = nodes_ext[i, :, cut]
            mixed[of] = (dot(spread_hi[...], part) + dot(spread_lo[...], part)).astype(BF16)
            if c == chunks - 1:
                decode(i, cut)
        if c < chunks - 1:

            @pl.loop(0, chunks)
            def _(n):
                term = dot(mixed[...], w_in[cut, at(n)])
                slope[:, at(n)] = term if c == 0 else slope[:, at(n)] + term

    def turn(c):
        cut = slice(c * STEP, (c + 1) * STEP)
        w_in_turned[:, cut] = w_in[cut, :].T

    for c in range(chunks // 2):
        turn(c)

    tile_shape = tiles.shape[1:]
    tile_row = lax.broadcasted_iota(jnp.int32, tile_shape, 0)
    tile_lane = lax.broadcasted_iota(jnp.int32, tile_shape, 1)

    def total(array):
        return jnp.sum(jnp.sum(array, axis=0, keepdims=True), axis=1, keepdims=True)

    def distance(a, b):
        gap = a - b
        return total(gap * gap)

    tile = jnp.where(tile_lane == members + 1, total(valid), 0.0)
    if members <= 4:
        order = [lax.rem(first + k, members) for k in range(members)]
        for a in range(members):
            if a == members_dev:
                for copy in field_copies:
                    copy.wait_recv()
            m = order[a]
            masked[m] = fields_all[m].astype(F32) * valid
            place = (tile_row == m) & (tile_lane == members)
            tile = jnp.where(place, distance(masked[m], target[...]), tile)
            for n in order[:a]:
                place = ((tile_row == m) & (tile_lane == n)) | ((tile_row == n) & (tile_lane == m))
                tile = jnp.where(place, distance(masked[m], masked[n]), tile)
    else:
        for copy in field_copies:
            copy.wait_recv()
        for m in range(members):
            masked[m] = fields_all[m].astype(F32) * valid

        def one_member(m, tile):
            own = masked[m]
            here = tile_row == m
            tile = jnp.where(here & (tile_lane == members), distance(own, target[...]), tile)
            return lax.fori_loop(
                0,
                members,
                lambda n, t: jnp.where(here & (tile_lane == n), distance(own, masked[n]), t),
                tile,
            )

        tile = lax.fori_loop(0, members, one_member, tile)
    tiles[band] = tile
    tile_copies = []
    for k in range(1, bands):
        copy = remote(
            tiles.at[band],
            tiles.at[band],
            tile_send.at[k - 1],
            tile_recv.at[k - 1],
            (mine, lax.rem(band + k, bands)),
        )
        copy.start()
        tile_copies.append(copy)
    for c in range(chunks // 2, chunks):
        turn(c)
    for copy in tile_copies:
        copy.wait_recv()
    summed = tiles[0]
    for k in range(1, bands):
        summed = summed + tiles[k]

    cells = variables * summed[0:1, members + 1 : members + 2]
    dist = jnp.sqrt(summed / cells + EPSILON)
    in_rows = tile_row < members
    pair = in_rows & (tile_lane < members) & (tile_row != tile_lane)
    own_lane = in_rows & (tile_lane == members)
    score_ref[...] = total(jnp.where(own_lane, dist, 0.0)) / members - total(
        jnp.where(pair, dist, 0.0)
    ) / (2.0 * members * (members - 1))
    inverse = 1.0 / dist
    pair_coef = jnp.where(pair, inverse / (members * (members - 1)), 0.0)
    coef_sum = jnp.sum(pair_coef, axis=1, keepdims=True)
    coefs[...] = jnp.where(
        own_lane, inverse / members, jnp.where(tile_lane == members + 1, coef_sum, pair_coef)
    )
    for i in range(members_dev):
        row = coefs[pl.ds(first + i, 1), :]
        own = masked[first + i]
        others = row[:, 0:1] * masked[0]
        for n in range(1, members):
            others = others + row[:, n : n + 1] * masked[n]
        toward = (own - target[...]) * row[:, members : members + 1]
        grad = toward - (row[:, members + 1 : members + 2] * own - others)
        grad_fields[i, 0:var_rows, :] = grad
        grad_fields[i, var_rows:, :] = jnp.zeros((grad_fields.shape[1] - var_rows, rows), F32)

    half_rows = weight_half.shape[1]
    half = lax.rem(rank, 2)

    @pl.loop(0, chunks)
    def _(c):
        part = dot(grad_fields[0, 0:var_rows, :].astype(BF16), hidden[0:rows, at(c)])
        for i in range(1, members_dev):
            part = part + dot(
                grad_fields[i, 0:var_rows, :].astype(BF16), hidden[i * rows : (i + 1) * rows, at(c)]
            )
        for j in range(STEP // LANES):
            for side in range(2):
                weight_blocks[side, c * (STEP // LANES) + j] = part[
                    side * half_rows : (side + 1) * half_rows, j * LANES : (j + 1) * LANES
                ]

    peer_copy = remote(
        weight_blocks.at[1 - half], weight_peer, peer_send, peer_recv, (mine, band + 1 - 2 * half)
    )
    peer_copy.start()
    part_copies = []
    for k in range(1, blocks):
        there = lax.rem(block + k, blocks)
        part_copies.append(
            remote(
                weight_half.at[there],
                weight_parts.at[block],
                part_send.at[k - 1],
                part_recv.at[k - 1],
                (mine, there * ranks + rank),
            )
        )

    side_rows = members_dev * nodes
    turned_grads = [grad_fields[i].T.astype(BF16) for i in range(members_dev)]
    rim_down, rim_up = [], []
    for c in range(chunks):
        cut = slice(c * STEP, (c + 1) * STEP)
        for i in range(members_dev):
            back = dot(turned_grads[i], w_out[:, cut])
            grad_pre = (back * slope[i * rows : (i + 1) * rows, cut]).astype(BF16)
            terms = dot(collect[...], grad_pre)
            gathered = terms[0:sides_rows] + terms[sides_rows:]
            of = slice(i * nodes, (i + 1) * nodes)
            rims[0, c, of] = gathered[0:nodes].astype(BF16)
            node_pre[of, cut] = gathered[nodes : 2 * nodes]
            rims[1, c, of] = gathered[2 * nodes :].astype(BF16)
        rim_down.append(
            remote(rims.at[0, c], rims_in.at[1, c], rim_send.at[0, c], rim_recv.at[0, c], (mine, band - 1))
        )
        rim_up.append(
            remote(rims.at[1, c], rims_in.at[0, c], rim_send.at[1, c], rim_recv.at[1, c], (mine, band + 1))
        )

        @pl.when(band > 0)
        def _():
            rim_down[c].start()

        @pl.when(band < bands - 1)
        def _():
            rim_up[c].start()

        if c == min(1, chunks - 1):
            peer_copy.wait_recv()
            weight_half[...] = weight_blocks[half] + weight_peer[...]
            for copy in part_copies:
                copy.start()
            weight_parts[block] = weight_half[block]

    for c in range(chunks):

        @pl.when(band < bands - 1)
        def _():
            rim_down[c].wait_recv()

        @pl.when(band > 0)
        def _():
            rim_up[c].wait_recv()

        cut = slice(c * STEP, (c + 1) * STEP)
        node_sum = node_pre[:, cut] + rims_in[1, c].astype(F32) + rims_in[0, c].astype(F32)
        term = dot(node_sum.astype(BF16), w_in_turned[cut, :])
        node_own[...] = term if c == 0 else node_own[...] + term

    for copy in part_copies:
        copy.wait_recv()
    part = weight_parts[0]
    for j in range(1, blocks):
        part = part + weight_parts[j]
    replicas = groups * ranks
    replica = mine * ranks + rank
    weight_sums[replica] = part
    sum_copies = []
    for k in range(1, replicas):
        there = lax.rem(replica + k, replicas)
        copy = remote(
            weight_sums.at[replica],
            weight_sums.at[replica],
            sum_send.at[k - 1],
            sum_recv.at[k - 1],
            (there // ranks, block * ranks + lax.rem(there, ranks)),
        )
        copy.start()
        sum_copies.append(copy)

    grad_latent_ref[...] = node_own[...].astype(BF16).reshape(members_dev, nodes, width)

    for copy in sum_copies:
        copy.wait_recv()
    sides = []
    for side in range(2):
        places = [k for k in range(replicas) if k % ranks % 2 == side]
        side_sum = weight_sums[places[0]]
        for k in places[1:]:
            side_sum = side_sum + weight_sums[k]
        sides.append(side_sum)
    sides.append(jnp.zeros((LANES - 2 * half_rows, LANES), F32))
    grad_out = jnp.concatenate(sides, axis=0).T
    columns = width // bands
    chosen = grad_out[0:columns]
    for other in range(1, ranks):
        chosen = jnp.where(rank == other, grad_out[other * columns : (other + 1) * columns], chosen)
    grad_w_out_ref[...] = chosen[:, 0:variables]

    for copy in field_copies + tile_copies + [peer_copy] + part_copies + sum_copies:
        copy.wait_send()
    for c in range(chunks):

        @pl.when(band < bands - 1)
        def _():
            halo_up[c].wait_send()
            rim_up[c].wait_send()

        @pl.when(band > 0)
        def _():
            halo_down[c].wait_send()
            rim_down[c].wait_send()


def hand_out(score_in, latent_in, weight_in, score_out, latent_out, weight_out):
    score_out[...] = score_in[...]
    latent_out[...] = latent_in[...]
    weight_out[...] = weight_in[...]


def per_device(latent, edge_weight, neighbours, band_rows, w_in, w_out, target):
    groups, bands = lax.axis_size("member"), lax.axis_size("space")
    members_dev, nodes, width = latent.shape
    rows = edge_weight.shape[1]
    variables = w_out.shape[0]
    members = groups * members_dev
    blocks = width // LANES
    replicas = groups * (bands // blocks)
    var_rows = round_up(variables, 16)
    chunks = width // STEP
    ext = round_up(3 * nodes, 256)
    vmem = pl.BlockSpec(memory_space=pltpu.VMEM)
    dma = pltpu.SemaphoreType.DMA
    score, grad_latent, grad_w_out = pl.pallas_call(
        functools.partial(kernel, (groups, bands)),
        out_shape=(
            jax.ShapeDtypeStruct((1, 1), F32),
            jax.ShapeDtypeStruct(latent.shape, BF16),
            jax.ShapeDtypeStruct((width // bands, variables), F32),
        ),
        in_specs=[pl.BlockSpec(memory_space=pltpu.HBM)] * 7,
        out_specs=(vmem, vmem, vmem),
        scratch_shapes=[
            pltpu.VMEM(edge_weight.shape, F32),
            pltpu.VMEM(neighbours.shape, jnp.int32),
            pltpu.SMEM(band_rows.shape, jnp.int32),
            pltpu.VMEM(w_out.shape, BF16),
            pltpu.VMEM(target.shape, F32),
            pltpu.VMEM((width, width), BF16),
            pltpu.VMEM((width, width), BF16),
            pltpu.VMEM((LANES, width), BF16),
            pltpu.VMEM((width, LANES), BF16),
            pltpu.VMEM((members_dev, ext, width), BF16),
            pltpu.VMEM((rows, ext), BF16),
            pltpu.VMEM((rows, ext), BF16),
            pltpu.VMEM((2 * 3 * nodes, rows), BF16),
            pltpu.VMEM((members_dev * rows, STEP), BF16),
            pltpu.VMEM((members_dev * rows, width), BF16),
            pltpu.VMEM((members_dev * rows, width), F32),
            pltpu.VMEM((members, var_rows, rows), BF16),
            pltpu.VMEM((members, var_rows, rows), F32),
            pltpu.VMEM((var_rows, rows), F32),
            pltpu.VMEM((bands, members, LANES), F32),
            pltpu.VMEM((members, LANES), F32),
            pltpu.VMEM((members_dev, LANES, rows), F32),
            pltpu.VMEM((2, blocks, var_rows // 2, LANES), F32),
            pltpu.VMEM((blocks, var_rows // 2, LANES), F32),
            pltpu.VMEM((blocks, var_rows // 2, LANES), F32),
            pltpu.VMEM((blocks, var_rows // 2, LANES), F32),
            pltpu.VMEM((replicas, var_rows // 2, LANES), F32),
            pltpu.VMEM((members_dev * nodes, width), F32),
            pltpu.VMEM((members_dev * nodes, width), F32),
            pltpu.VMEM((2, chunks, members_dev * nodes, STEP), BF16),
            pltpu.VMEM((2, chunks, members_dev * nodes, STEP), BF16),
            dma((7,)),
            dma((2, chunks)),
            dma((2, chunks)),
            dma((max(groups - 1, 1), members_dev)),
            dma((max(groups - 1, 1), members_dev)),
            dma((bands - 1,)),
            dma((bands - 1,)),
            dma,
            dma,
            dma((blocks - 1,)),
            dma((blocks - 1,)),
            dma((replicas - 1,)),
            dma((replicas - 1,)),
            dma((2, chunks)),
            dma((2, chunks)),
        ],
        compiler_params=pltpu.CompilerParams(
            collective_id=0, has_side_effects=True, vmem_limit_bytes=40 * 1024 * 1024
        ),
        name="decoder",
    )(latent, edge_weight, neighbours, band_rows, w_in, w_out, target)
    shapes = (score, grad_latent, grad_w_out)
    score, grad_latent, grad_w_out = pl.pallas_call(
        hand_out,
        out_shape=tuple(jax.ShapeDtypeStruct(a.shape, a.dtype) for a in shapes),
        in_specs=[vmem] * 3,
        out_specs=(vmem,) * 3,
        name="hand_out",
    )(score, grad_latent, grad_w_out)
    return (score[0, 0], grad_latent, grad_w_out.T)


def solution(mesh):
    return jax.shard_map(
        per_device,
        mesh=mesh,
        in_specs=(
            P("member", "space", None),
            P(None, "space"),
            P(None, "space"),
            P("space"),
            P(),
            P(),
            P(None, "space"),
        ),
        out_specs=(P(), P("member", "space", None), P(None, "space")),
        check_vma=False,
    )
```

```python
import functools

import jax
import jax.numpy as jnp
from jax import lax
from jax.experimental import pallas as pl
from jax.experimental.pallas import tpu as pltpu
from jax.sharding import PartitionSpec as P

EPSILON = 1e-06
MESH = pl.DeviceIdType.MESH
F32 = jnp.float32
BF16 = jnp.bfloat16
LANES = 128
STEP = 256


def round_up(value, unit):
    return -(-value // unit) * unit


def dot(a, b, over=((1,), (0,))):
    return lax.dot_general(a, b, (over, ((), ())), preferred_element_type=F32)


def kernel(
    sizes,
    latent_ref,
    edge_weight_hbm,
    neighbours_hbm,
    band_rows_hbm,
    w_in_hbm,
    w_out_hbm,
    target_hbm,
    score_ref,
    grad_latent_ref,
    grad_w_out_ref,
    edge_weight_ref,
    neighbours_ref,
    band_rows_ref,
    w_out_ref,
    target_ref,
    w_in,
    w_in_turned,
    w_out,
    w_out_turned,
    nodes_ext,
    spread_hi,
    spread_lo,
    collect,
    mixed,
    hidden,
    slope,
    fields_all,
    masked,
    target,
    tiles,
    coefs,
    grad_fields,
    weight_blocks,
    weight_parts,
    weight_sums,
    node_pre,
    node_own,
    rims,
    rims_in,
    load_sem,
    halo_send,
    halo_recv,
    field_send,
    field_recv,
    tile_send,
    tile_recv,
    part_send,
    part_recv,
    sum_send,
    sum_recv,
    rim_send,
    rim_recv,
):
    groups, bands = sizes
    members_dev, nodes, width = latent_ref.shape
    neigh, rows = edge_weight_ref.shape
    variables = w_out_ref.shape[0]
    members = groups * members_dev
    var_rows = fields_all.shape[1]
    blocks = width // LANES
    ranks = bands // blocks
    mine = lax.axis_index("member")
    band = lax.axis_index("space")
    block = band // ranks
    rank = lax.rem(band, ranks)

    barrier = pltpu.get_barrier_semaphore()
    partners = [(mine, lax.rem(band + k, bands)) for k in range(1, bands)]
    for k in range(1, groups):
        for other in range(ranks):
            partners.append((lax.rem(mine + k, groups), block * ranks + other))
    for partner in partners:
        pl.semaphore_signal(barrier, inc=1, device_id=partner, device_id_type=MESH)

    loads = [
        pltpu.make_async_copy(src, dst, load_sem.at[k])
        for k, (src, dst) in enumerate(
            (
                (edge_weight_hbm, edge_weight_ref),
                (neighbours_hbm, neighbours_ref),
                (latent_ref, nodes_ext.at[:, pl.ds(nodes, nodes)]),
                (band_rows_hbm, band_rows_ref),
                (target_hbm, target_ref),
                (w_out_hbm, w_out_ref),
                (w_in_hbm, w_in),
            )
        )
    ]
    for load in loads:
        load.start()
    pl.semaphore_wait(barrier, len(partners))
    chunks = width // STEP

    def remote(src, dst, send, recv, device):
        return pltpu.make_async_remote_copy(
            src_ref=src, dst_ref=dst, send_sem=send, recv_sem=recv, device_id=device, device_id_type=MESH
        )

    halo_up, halo_down = [], []
    for c in range(chunks):
        cut = pl.ds(c * STEP, STEP)
        for way, copies, low in ((0, halo_up, 0), (1, halo_down, 2 * nodes)):
            copies.append(
                remote(
                    latent_ref.at[:, :, cut],
                    nodes_ext.at[:, pl.ds(low, nodes), cut],
                    halo_send.at[way, c],
                    halo_recv.at[way, c],
                    (mine, band + 1 - 2 * way),
                )
            )
    for c in range(chunks):

        @pl.when(band < bands - 1)
        def _():
            halo_up[c].start()

        @pl.when(band > 0)
        def _():
            halo_down[c].start()

    @pl.when(band == 0)
    def _():
        nodes_ext[:, 0:nodes, :] = jnp.zeros((members_dev, nodes, width), BF16)
        rims_in[0] = jnp.zeros(rims_in.shape[1:], BF16)

    @pl.when(band == bands - 1)
    def _():
        nodes_ext[:, 2 * nodes : 3 * nodes, :] = jnp.zeros((members_dev, nodes, width), BF16)
        rims_in[1] = jnp.zeros(rims_in.shape[1:], BF16)

    ext = nodes_ext.shape[1]
    nodes_ext[:, 3 * nodes :, :] = jnp.zeros((members_dev, ext - 3 * nodes, width), BF16)
    loads[0].wait()
    loads[1].wait()
    local = neighbours_ref[...] - (band - 1) * nodes
    node_id = lax.broadcasted_iota(jnp.int32, (ext, rows), 0)
    weights = jnp.zeros((ext, rows), F32)
    for k in range(neigh):
        weights = weights + jnp.where(node_id == local[k : k + 1, :], edge_weight_ref[k : k + 1, :], 0.0)
    high = weights.astype(BF16)
    sides_rows = 3 * nodes
    collect[0:sides_rows, :] = high[0:sides_rows]
    collect[sides_rows:, :] = (weights - high.astype(F32)).astype(BF16)[0:sides_rows]
    turned = weights.T
    high = turned.astype(BF16)
    spread_hi[...] = high
    spread_lo[...] = (turned - high.astype(F32)).astype(BF16)

    for k in range(2, 6):
        loads[k].wait()
    valid = (lax.broadcasted_iota(jnp.int32, (1, rows), 1) < band_rows_ref[0]).astype(F32)
    target[...] = jnp.zeros(target.shape, F32)
    target[0:variables, :] = target_ref[...] * valid
    w_out[...] = jnp.zeros(w_out.shape, BF16)
    w_out[0:variables, :] = w_out_ref[...]
    w_out_turned[...] = w_out[...].astype(F32).T.astype(BF16)

    def at(c):
        return pl.ds(pl.multiple_of(c * STEP, STEP), STEP)

    first = mine * members_dev
    field_copies = []

    def decode(i, cut):
        of = slice(i * rows, (i + 1) * rows)

        @pl.loop(0, chunks)
        def _(n):
            preact = slope[of, at(n)] + dot(mixed[of], w_in[cut, at(n)])
            sigmoid = 0.5 + 0.5 * jnp.tanh(0.5 * preact)
            hidden[of, at(n)] = (preact * sigmoid).astype(BF16)
            slope[of, at(n)] = sigmoid * (1.0 + preact * (1.0 - sigmoid))

        decoded = dot(hidden[of, :], w_out_turned[...])
        fields_all[first + i] = decoded.T[0:var_rows].astype(BF16)
        for k in range(1, groups):
            here = fields_all.at[first + i]
            copy = remote(
                here,
                here,
                field_send.at[k - 1, i],
                field_recv.at[k - 1, i],
                (lax.rem(mine + k, groups), band),
            )
            copy.start()
            field_copies.append(copy)

    for c in range(chunks):

        @pl.when(band > 0)
        def _():
            halo_up[c].wait_recv()

        @pl.when(band < bands - 1)
        def _():
            halo_down[c].wait_recv()

        if c == 0:
            loads[6].wait()
        cut = slice(c * STEP, (c + 1) * STEP)
        for i in range(members_dev):
            of = slice(i * rows, (i + 1) * rows)
            part = nodes_ext[i, :, cut]
            mixed[of] = (dot(spread_hi[...], part) + dot(spread_lo[...], part)).astype(BF16)
            if c == chunks - 1:
                decode(i, cut)
        if c < chunks - 1:

            @pl.loop(0, chunks)
            def _(n):
                term = dot(mixed[...], w_in[cut, at(n)])
                slope[:, at(n)] = term if c == 0 else slope[:, at(n)] + term

    def turn(c):
        cut = slice(c * STEP, (c + 1) * STEP)
        w_in_turned[:, cut] = w_in[cut, :].T

    for c in range(chunks // 2):
        turn(c)

    tile_shape = tiles.shape[1:]
    tile_row = lax.broadcasted_iota(jnp.int32, tile_shape, 0)
    tile_lane = lax.broadcasted_iota(jnp.int32, tile_shape, 1)

    def total(array):
        return jnp.sum(jnp.sum(array, axis=0, keepdims=True), axis=1, keepdims=True)

    def distance(a, b):
        gap = a - b
        square = gap * gap
        folded = square[:, 0:LANES]
        for k in range(1, rows // LANES):
            folded = folded + square[:, k * LANES : (k + 1) * LANES]
        return total(folded)

    tile = jnp.where(tile_lane == members + 1, total(valid), 0.0)
    if members <= 4:
        order = [lax.rem(first + k, members) for k in range(members)]
        for a in range(members):
            if a == members_dev:
                for copy in field_copies:
                    copy.wait_recv()
            m = order[a]
            masked[m] = fields_all[m].astype(F32) * valid
            place = (tile_row == m) & (tile_lane == members)
            tile = jnp.where(place, distance(masked[m], target[...]), tile)
            for n in order[:a]:
                place = ((tile_row == m) & (tile_lane == n)) | ((tile_row == n) & (tile_lane == m))
                tile = jnp.where(place, distance(masked[m], masked[n]), tile)
    else:
        for copy in field_copies:
            copy.wait_recv()
        for m in range(members):
            masked[m] = fields_all[m].astype(F32) * valid

        def one_member(m, tile):
            own = masked[m]
            here = tile_row == m
            tile = jnp.where(here & (tile_lane == members), distance(own, target[...]), tile)
            return lax.fori_loop(
                0,
                members,
                lambda n, t: jnp.where(here & (tile_lane == n), distance(own, masked[n]), t),
                tile,
            )

        tile = lax.fori_loop(0, members, one_member, tile)
    tiles[band] = tile
    tile_copies = []
    for k in range(1, bands):
        copy = remote(
            tiles.at[band],
            tiles.at[band],
            tile_send.at[k - 1],
            tile_recv.at[k - 1],
            (mine, lax.rem(band + k, bands)),
        )
        copy.start()
        tile_copies.append(copy)
    for c in range(chunks // 2, chunks):
        turn(c)
    for copy in tile_copies:
        copy.wait_recv()
    summed = tiles[0]
    for k in range(1, bands):
        summed = summed + tiles[k]

    cells = variables * summed[0:1, members + 1 : members + 2]
    dist = jnp.sqrt(summed / cells + EPSILON)
    in_rows = tile_row < members
    pair = in_rows & (tile_lane < members) & (tile_row != tile_lane)
    own_lane = in_rows & (tile_lane == members)
    score_ref[...] = total(jnp.where(own_lane, dist, 0.0)) / members - total(
        jnp.where(pair, dist, 0.0)
    ) / (2.0 * members * (members - 1))
    inverse = 1.0 / dist
    pair_coef = jnp.where(pair, inverse / (members * (members - 1)), 0.0)
    coef_sum = jnp.sum(pair_coef, axis=1, keepdims=True)
    coefs[...] = jnp.where(
        own_lane, inverse / members, jnp.where(tile_lane == members + 1, coef_sum, pair_coef)
    )
    for i in range(members_dev):
        row = coefs[pl.ds(first + i, 1), :]
        own = masked[first + i]
        others = row[:, 0:1] * masked[0]
        for n in range(1, members):
            others = others + row[:, n : n + 1] * masked[n]
        toward = (own - target[...]) * row[:, members : members + 1]
        grad = toward - (row[:, members + 1 : members + 2] * own - others)
        grad_fields[i, 0:var_rows, :] = grad
        grad_fields[i, var_rows:, :] = jnp.zeros((grad_fields.shape[1] - var_rows, rows), F32)


    @pl.loop(0, chunks)
    def _(c):
        part = dot(grad_fields[0, 0:var_rows, :].astype(BF16), hidden[0:rows, at(c)])
        for i in range(1, members_dev):
            part = part + dot(
                grad_fields[i, 0:var_rows, :].astype(BF16), hidden[i * rows : (i + 1) * rows, at(c)]
            )
        for j in range(STEP // LANES):
            weight_blocks[c * (STEP // LANES) + j] = part[:, j * LANES : (j + 1) * LANES].astype(BF16)

    part_copies = []
    for k in range(1, blocks):
        there = lax.rem(block + k, blocks)
        copy = remote(
            weight_blocks.at[there],
            weight_parts.at[block],
            part_send.at[k - 1],
            part_recv.at[k - 1],
            (mine, there * ranks + rank),
        )
        copy.start()
        part_copies.append(copy)
    weight_parts[block] = weight_blocks[block]

    side_rows = members_dev * nodes
    turned_grads = [grad_fields[i].T.astype(BF16) for i in range(members_dev)]
    rim_down, rim_up = [], []
    for c in range(chunks):
        cut = slice(c * STEP, (c + 1) * STEP)
        for i in range(members_dev):
            back = dot(turned_grads[i], w_out[:, cut])
            grad_pre = (back * slope[i * rows : (i + 1) * rows, cut]).astype(BF16)
            terms = dot(collect[...], grad_pre)
            gathered = terms[0:sides_rows] + terms[sides_rows:]
            of = slice(i * nodes, (i + 1) * nodes)
            rims[0, c, of] = gathered[0:nodes].astype(BF16)
            node_pre[of, cut] = gathered[nodes : 2 * nodes]
            rims[1, c, of] = gathered[2 * nodes :].astype(BF16)
        rim_down.append(
            remote(rims.at[0, c], rims_in.at[1, c], rim_send.at[0, c], rim_recv.at[0, c], (mine, band - 1))
        )
        rim_up.append(
            remote(rims.at[1, c], rims_in.at[0, c], rim_send.at[1, c], rim_recv.at[1, c], (mine, band + 1))
        )

        @pl.when(band > 0)
        def _():
            rim_down[c].start()

        @pl.when(band < bands - 1)
        def _():
            rim_up[c].start()

    replicas = groups * ranks
    sum_copies = []

    def share():
        for copy in part_copies:
            copy.wait_recv()
        part = weight_parts[0].astype(F32)
        for j in range(1, blocks):
            part = part + weight_parts[j].astype(F32)
        replica = mine * ranks + rank
        weight_sums[replica] = part
        for k in range(1, replicas):
            there = lax.rem(replica + k, replicas)
            copy = remote(
                weight_sums.at[replica],
                weight_sums.at[replica],
                sum_send.at[k - 1],
                sum_recv.at[k - 1],
                (there // ranks, block * ranks + lax.rem(there, ranks)),
            )
            copy.start()
            sum_copies.append(copy)

    for c in range(chunks):

        @pl.when(band < bands - 1)
        def _():
            rim_down[c].wait_recv()

        @pl.when(band > 0)
        def _():
            rim_up[c].wait_recv()

        cut = slice(c * STEP, (c + 1) * STEP)
        node_sum = node_pre[:, cut] + rims_in[1, c].astype(F32) + rims_in[0, c].astype(F32)
        term = dot(node_sum.astype(BF16), w_in_turned[cut, :])
        node_own[...] = term if c == 0 else node_own[...] + term
        if c == 1:
            share()

    grad_latent_ref[...] = node_own[...].astype(BF16).reshape(members_dev, nodes, width)

    for copy in sum_copies:
        copy.wait_recv()
    grad_sum = weight_sums[0]
    for k in range(1, replicas):
        grad_sum = grad_sum + weight_sums[k]
    unused = jnp.zeros((LANES - var_rows, LANES), F32)
    grad_out = jnp.concatenate([grad_sum, unused], axis=0).T
    columns = width // bands
    chosen = grad_out[0:columns]
    for other in range(1, ranks):
        chosen = jnp.where(rank == other, grad_out[other * columns : (other + 1) * columns], chosen)
    grad_w_out_ref[...] = chosen[:, 0:variables]

    for copy in field_copies + tile_copies + part_copies + sum_copies:
        copy.wait_send()
    for c in range(chunks):

        @pl.when(band < bands - 1)
        def _():
            halo_up[c].wait_send()
            rim_up[c].wait_send()

        @pl.when(band > 0)
        def _():
            halo_down[c].wait_send()
            rim_down[c].wait_send()


def per_device(latent, edge_weight, neighbours, band_rows, w_in, w_out, target):
    groups, bands = lax.axis_size("member"), lax.axis_size("space")
    members_dev, nodes, width = latent.shape
    rows = edge_weight.shape[1]
    variables = w_out.shape[0]
    members = groups * members_dev
    blocks = width // LANES
    replicas = groups * (bands // blocks)
    var_rows = round_up(variables, 16)
    chunks = width // STEP
    ext = round_up(3 * nodes, 256)
    vmem = pl.BlockSpec(memory_space=pltpu.VMEM)
    dma = pltpu.SemaphoreType.DMA
    score, grad_latent, grad_w_out = pl.pallas_call(
        functools.partial(kernel, (groups, bands)),
        out_shape=(
            jax.ShapeDtypeStruct((1, 1), F32),
            jax.ShapeDtypeStruct(latent.shape, BF16),
            jax.ShapeDtypeStruct((width // bands, variables), F32),
        ),
        in_specs=[pl.BlockSpec(memory_space=pltpu.HBM)] * 7,
        out_specs=(vmem, vmem, vmem),
        scratch_shapes=[
            pltpu.VMEM(edge_weight.shape, F32),
            pltpu.VMEM(neighbours.shape, jnp.int32),
            pltpu.SMEM(band_rows.shape, jnp.int32),
            pltpu.VMEM(w_out.shape, BF16),
            pltpu.VMEM(target.shape, F32),
            pltpu.VMEM((width, width), BF16),
            pltpu.VMEM((width, width), BF16),
            pltpu.VMEM((LANES, width), BF16),
            pltpu.VMEM((width, LANES), BF16),
            pltpu.VMEM((members_dev, ext, width), BF16),
            pltpu.VMEM((rows, ext), BF16),
            pltpu.VMEM((rows, ext), BF16),
            pltpu.VMEM((2 * 3 * nodes, rows), BF16),
            pltpu.VMEM((members_dev * rows, STEP), BF16),
            pltpu.VMEM((members_dev * rows, width), BF16),
            pltpu.VMEM((members_dev * rows, width), F32),
            pltpu.VMEM((members, var_rows, rows), BF16),
            pltpu.VMEM((members, var_rows, rows), F32),
            pltpu.VMEM((var_rows, rows), F32),
            pltpu.VMEM((bands, members, LANES), F32),
            pltpu.VMEM((members, LANES), F32),
            pltpu.VMEM((members_dev, LANES, rows), F32),
            pltpu.VMEM((blocks, var_rows, LANES), BF16),
            pltpu.VMEM((blocks, var_rows, LANES), BF16),
            pltpu.VMEM((replicas, var_rows, LANES), F32),
            pltpu.VMEM((members_dev * nodes, width), F32),
            pltpu.VMEM((members_dev * nodes, width), F32),
            pltpu.VMEM((2, chunks, members_dev * nodes, STEP), BF16),
            pltpu.VMEM((2, chunks, members_dev * nodes, STEP), BF16),
            dma((7,)),
            dma((2, chunks)),
            dma((2, chunks)),
            dma((max(groups - 1, 1), members_dev)),
            dma((max(groups - 1, 1), members_dev)),
            dma((bands - 1,)),
            dma((bands - 1,)),
            dma((blocks - 1,)),
            dma((blocks - 1,)),
            dma((replicas - 1,)),
            dma((replicas - 1,)),
            dma((2, chunks)),
            dma((2, chunks)),
        ],
        compiler_params=pltpu.CompilerParams(
            collective_id=0, has_side_effects=True, vmem_limit_bytes=60 * 1024 * 1024
        ),
        name="decoder",
    )(latent, edge_weight, neighbours, band_rows, w_in, w_out, target)
    return (score[0, 0], grad_latent, grad_w_out.T)


def solution(mesh):
    return jax.shard_map(
        per_device,
        mesh=mesh,
        in_specs=(
            P("member", "space", None),
            P(None, "space"),
            P(None, "space"),
            P("space"),
            P(),
            P(),
            P(None, "space"),
        ),
        out_specs=(P(), P("member", "space", None), P(None, "space")),
        check_vma=False,
    )
```

```python
import functools

import jax
import jax.numpy as jnp
from jax import lax
from jax.experimental import pallas as pl
from jax.experimental.pallas import tpu as pltpu
from jax.sharding import PartitionSpec as P

EPSILON = 1e-06
MESH = pl.DeviceIdType.MESH
F32 = jnp.float32
BF16 = jnp.bfloat16
LANES = 128
STEP = 256


def round_up(value, unit):
    return -(-value // unit) * unit


def dot(a, b, over=((1,), (0,))):
    return lax.dot_general(a, b, (over, ((), ())), preferred_element_type=F32)


def kernel(
    sizes,
    latent_ref,
    edge_weight_hbm,
    neighbours_hbm,
    band_rows_hbm,
    w_in_hbm,
    w_out_hbm,
    target_hbm,
    score_ref,
    grad_latent_ref,
    grad_w_out_ref,
    edge_weight_ref,
    neighbours_ref,
    band_rows_ref,
    w_out_ref,
    target_ref,
    w_in,
    w_in_turned,
    w_out,
    w_out_turned,
    nodes_ext,
    spread_hi,
    spread_lo,
    collect,
    mixed,
    hidden,
    slope,
    fields_all,
    masked,
    target,
    tiles,
    coefs,
    grad_fields,
    weight_blocks,
    weight_parts,
    weight_sums,
    node_pre,
    node_own,
    rims,
    rims_in,
    load_sem,
    halo_send,
    halo_recv,
    field_send,
    field_recv,
    tile_send,
    tile_recv,
    part_send,
    part_recv,
    sum_send,
    sum_recv,
    rim_send,
    rim_recv,
):
    groups, bands = sizes
    members_dev, nodes, width = latent_ref.shape
    neigh, rows = edge_weight_ref.shape
    variables = w_out_ref.shape[0]
    members = groups * members_dev
    var_rows = fields_all.shape[1]
    blocks = width // LANES
    ranks = bands // blocks
    mine = lax.axis_index("member")
    band = lax.axis_index("space")
    block = band // ranks
    rank = lax.rem(band, ranks)

    barrier = pltpu.get_barrier_semaphore()
    partners = [(mine, lax.rem(band + k, bands)) for k in range(1, bands)]
    for k in range(1, groups):
        for other in range(ranks):
            partners.append((lax.rem(mine + k, groups), block * ranks + other))
    for partner in partners:
        pl.semaphore_signal(barrier, inc=1, device_id=partner, device_id_type=MESH)

    loads = [
        pltpu.make_async_copy(src, dst, load_sem.at[k])
        for k, (src, dst) in enumerate(
            (
                (edge_weight_hbm, edge_weight_ref),
                (neighbours_hbm, neighbours_ref),
                (latent_ref, nodes_ext.at[:, pl.ds(nodes, nodes)]),
                (band_rows_hbm, band_rows_ref),
                (target_hbm, target_ref),
                (w_out_hbm, w_out_ref),
                (w_in_hbm, w_in),
            )
        )
    ]
    for load in loads:
        load.start()
    pl.semaphore_wait(barrier, len(partners))
    chunks = width // STEP

    def remote(src, dst, send, recv, device):
        return pltpu.make_async_remote_copy(
            src_ref=src, dst_ref=dst, send_sem=send, recv_sem=recv, device_id=device, device_id_type=MESH
        )

    halo_up, halo_down = [], []
    for c in range(chunks):
        cut = pl.ds(c * STEP, STEP)
        for way, copies, low in ((0, halo_up, 0), (1, halo_down, 2 * nodes)):
            copies.append(
                remote(
                    latent_ref.at[:, :, cut],
                    nodes_ext.at[:, pl.ds(low, nodes), cut],
                    halo_send.at[way, c],
                    halo_recv.at[way, c],
                    (mine, band + 1 - 2 * way),
                )
            )
    for c in range(chunks):

        @pl.when(band < bands - 1)
        def _():
            halo_up[c].start()

        @pl.when(band > 0)
        def _():
            halo_down[c].start()

    @pl.when(band == 0)
    def _():
        nodes_ext[:, 0:nodes, :] = jnp.zeros((members_dev, nodes, width), BF16)
        rims_in[0] = jnp.zeros(rims_in.shape[1:], BF16)

    @pl.when(band == bands - 1)
    def _():
        nodes_ext[:, 2 * nodes : 3 * nodes, :] = jnp.zeros((members_dev, nodes, width), BF16)
        rims_in[1] = jnp.zeros(rims_in.shape[1:], BF16)

    ext = nodes_ext.shape[1]
    nodes_ext[:, 3 * nodes :, :] = jnp.zeros((members_dev, ext - 3 * nodes, width), BF16)
    loads[0].wait()
    loads[1].wait()
    local = neighbours_ref[...] - (band - 1) * nodes
    node_id = lax.broadcasted_iota(jnp.int32, (ext, rows), 0)
    weights = jnp.zeros((ext, rows), F32)
    for k in range(neigh):
        weights = weights + jnp.where(node_id == local[k : k + 1, :], edge_weight_ref[k : k + 1, :], 0.0)
    high = weights.astype(BF16)
    sides_rows = 3 * nodes
    collect[0:sides_rows, :] = high[0:sides_rows]
    collect[sides_rows:, :] = (weights - high.astype(F32)).astype(BF16)[0:sides_rows]
    turned = weights.T
    high = turned.astype(BF16)
    spread_hi[...] = high
    spread_lo[...] = (turned - high.astype(F32)).astype(BF16)

    for k in range(2, 6):
        loads[k].wait()
    valid = (lax.broadcasted_iota(jnp.int32, (1, rows), 1) < band_rows_ref[0]).astype(F32)
    target[...] = jnp.zeros(target.shape, F32)
    target[0:variables, :] = target_ref[...] * valid
    w_out[...] = jnp.zeros(w_out.shape, BF16)
    w_out[0:variables, :] = w_out_ref[...]
    w_out_turned[...] = w_out[...].astype(F32).T.astype(BF16)

    def at(c):
        return pl.ds(pl.multiple_of(c * STEP, STEP), STEP)

    first = mine * members_dev
    field_copies = []

    def decode(i, cut):
        of = slice(i * rows, (i + 1) * rows)

        @pl.loop(0, chunks)
        def _(n):
            preact = slope[of, at(n)] + dot(mixed[of], w_in[cut, at(n)])
            sigmoid = 0.5 + 0.5 * jnp.tanh(0.5 * preact)
            hidden[of, at(n)] = (preact * sigmoid).astype(BF16)
            slope[of, at(n)] = sigmoid * (1.0 + preact * (1.0 - sigmoid))

        decoded = dot(hidden[of, :], w_out_turned[...])
        fields_all[first + i] = decoded.T[0:var_rows].astype(BF16)
        for k in range(1, groups):
            here = fields_all.at[first + i]
            copy = remote(
                here,
                here,
                field_send.at[k - 1, i],
                field_recv.at[k - 1, i],
                (lax.rem(mine + k, groups), band),
            )
            copy.start()
            field_copies.append(copy)

    for c in range(chunks):

        @pl.when(band > 0)
        def _():
            halo_up[c].wait_recv()

        @pl.when(band < bands - 1)
        def _():
            halo_down[c].wait_recv()

        if c == 0:
            loads[6].wait()
        cut = slice(c * STEP, (c + 1) * STEP)
        for i in range(members_dev):
            of = slice(i * rows, (i + 1) * rows)
            part = nodes_ext[i, :, cut]
            mixed[of] = (dot(spread_hi[...], part) + dot(spread_lo[...], part)).astype(BF16)
            if c == chunks - 1:
                decode(i, cut)
        if c < chunks - 1:

            @pl.loop(0, chunks)
            def _(n):
                term = dot(mixed[...], w_in[cut, at(n)])
                slope[:, at(n)] = term if c == 0 else slope[:, at(n)] + term

    def turn(c):
        cut = slice(c * STEP, (c + 1) * STEP)
        w_in_turned[cut, :] = w_in[:, cut].T

    tile_shape = tiles.shape[1:]
    tile_row = lax.broadcasted_iota(jnp.int32, tile_shape, 0)
    tile_lane = lax.broadcasted_iota(jnp.int32, tile_shape, 1)

    def total(array):
        return jnp.sum(jnp.sum(array, axis=0, keepdims=True), axis=1, keepdims=True)

    def distance(a, b):
        gap = a - b
        square = gap * gap
        folded = square[:, 0:LANES]
        for k in range(1, rows // LANES):
            folded = folded + square[:, k * LANES : (k + 1) * LANES]
        return total(folded)

    tile = jnp.where(tile_lane == members + 1, total(valid), 0.0)
    if members <= 4:
        order = [lax.rem(first + k, members) for k in range(members)]
        for a in range(members):
            if a == members_dev:
                turn(0)
                for copy in field_copies:
                    copy.wait_recv()
            m = order[a]
            masked[m] = fields_all[m].astype(F32) * valid
            place = (tile_row == m) & (tile_lane == members)
            tile = jnp.where(place, distance(masked[m], target[...]), tile)
            for n in order[:a]:
                place = ((tile_row == m) & (tile_lane == n)) | ((tile_row == n) & (tile_lane == m))
                tile = jnp.where(place, distance(masked[m], masked[n]), tile)
    else:
        turn(0)
        for copy in field_copies:
            copy.wait_recv()
        for m in range(members):
            masked[m] = fields_all[m].astype(F32) * valid

        def one_member(m, tile):
            own = masked[m]
            here = tile_row == m
            tile = jnp.where(here & (tile_lane == members), distance(own, target[...]), tile)
            return lax.fori_loop(
                0,
                members,
                lambda n, t: jnp.where(here & (tile_lane == n), distance(own, masked[n]), t),
                tile,
            )

        tile = lax.fori_loop(0, members, one_member, tile)
    tiles[band] = tile
    tile_copies = []
    for k in range(1, bands):
        copy = remote(
            tiles.at[band],
            tiles.at[band],
            tile_send.at[k - 1],
            tile_recv.at[k - 1],
            (mine, lax.rem(band + k, bands)),
        )
        copy.start()
        tile_copies.append(copy)
    turn(1)
    for copy in tile_copies:
        copy.wait_recv()
    summed = tiles[0]
    for k in range(1, bands):
        summed = summed + tiles[k]

    cells = variables * summed[0:1, members + 1 : members + 2]
    dist = jnp.sqrt(summed / cells + EPSILON)
    in_rows = tile_row < members
    pair = in_rows & (tile_lane < members) & (tile_row != tile_lane)
    own_lane = in_rows & (tile_lane == members)
    score_ref[...] = total(jnp.where(own_lane, dist, 0.0)) / members - total(
        jnp.where(pair, dist, 0.0)
    ) / (2.0 * members * (members - 1))
    inverse = 1.0 / dist
    pair_coef = jnp.where(pair, inverse / (members * (members - 1)), 0.0)
    coef_sum = jnp.sum(pair_coef, axis=1, keepdims=True)
    coefs[...] = jnp.where(
        own_lane, inverse / members, jnp.where(tile_lane == members + 1, coef_sum, pair_coef)
    )
    for i in range(members_dev):
        row = coefs[pl.ds(first + i, 1), :]
        own = masked[first + i]
        others = row[:, 0:1] * masked[0]
        for n in range(1, members):
            others = others + row[:, n : n + 1] * masked[n]
        toward = (own - target[...]) * row[:, members : members + 1]
        grad = toward - (row[:, members + 1 : members + 2] * own - others)
        grad_fields[i, 0:var_rows, :] = grad
        grad_fields[i, var_rows:, :] = jnp.zeros((grad_fields.shape[1] - var_rows, rows), F32)


    @pl.loop(0, chunks)
    def _(c):
        part = dot(grad_fields[0, 0:var_rows, :].astype(BF16), hidden[0:rows, at(c)])
        for i in range(1, members_dev):
            part = part + dot(
                grad_fields[i, 0:var_rows, :].astype(BF16), hidden[i * rows : (i + 1) * rows, at(c)]
            )
        for j in range(STEP // LANES):
            weight_blocks[c * (STEP // LANES) + j] = part[:, j * LANES : (j + 1) * LANES].astype(BF16)

    part_copies = []
    for k in range(1, blocks):
        there = lax.rem(block + k, blocks)
        copy = remote(
            weight_blocks.at[there],
            weight_parts.at[block],
            part_send.at[k - 1],
            part_recv.at[k - 1],
            (mine, there * ranks + rank),
        )
        copy.start()
        part_copies.append(copy)
    weight_parts[block] = weight_blocks[block]

    side_rows = members_dev * nodes
    turned_grads = [grad_fields[i].T.astype(BF16) for i in range(members_dev)]
    rim_down, rim_up = [], []
    for c in range(chunks):
        cut = slice(c * STEP, (c + 1) * STEP)
        for i in range(members_dev):
            back = dot(turned_grads[i], w_out[:, cut])
            grad_pre = (back * slope[i * rows : (i + 1) * rows, cut]).astype(BF16)
            terms = dot(collect[...], grad_pre)
            gathered = terms[0:sides_rows] + terms[sides_rows:]
            of = slice(i * nodes, (i + 1) * nodes)
            rims[0, c, of] = gathered[0:nodes].astype(BF16)
            node_pre[of, cut] = gathered[nodes : 2 * nodes]
            rims[1, c, of] = gathered[2 * nodes :].astype(BF16)
        rim_down.append(
            remote(rims.at[0, c], rims_in.at[1, c], rim_send.at[0, c], rim_recv.at[0, c], (mine, band - 1))
        )
        rim_up.append(
            remote(rims.at[1, c], rims_in.at[0, c], rim_send.at[1, c], rim_recv.at[1, c], (mine, band + 1))
        )

        @pl.when(band > 0)
        def _():
            rim_down[c].start()

        @pl.when(band < bands - 1)
        def _():
            rim_up[c].start()

    replicas = groups * ranks
    sum_copies = []

    def share():
        for copy in part_copies:
            copy.wait_recv()
        part = weight_parts[0].astype(F32)
        for j in range(1, blocks):
            part = part + weight_parts[j].astype(F32)
        replica = mine * ranks + rank
        weight_sums[replica] = part
        for k in range(1, replicas):
            there = lax.rem(replica + k, replicas)
            copy = remote(
                weight_sums.at[replica],
                weight_sums.at[replica],
                sum_send.at[k - 1],
                sum_recv.at[k - 1],
                (there // ranks, block * ranks + lax.rem(there, ranks)),
            )
            copy.start()
            sum_copies.append(copy)

    for c in range(2, chunks):
        turn(c)
    for c in range(chunks):

        @pl.when(band < bands - 1)
        def _():
            rim_down[c].wait_recv()

        @pl.when(band > 0)
        def _():
            rim_up[c].wait_recv()

        cut = slice(c * STEP, (c + 1) * STEP)
        node_sum = node_pre[:, cut] + rims_in[1, c].astype(F32) + rims_in[0, c].astype(F32)
        term = dot(node_sum.astype(BF16), w_in_turned[cut, :])
        node_own[...] = term if c == 0 else node_own[...] + term
        if c == 1:
            share()

    grad_latent_ref[...] = node_own[...].astype(BF16).reshape(members_dev, nodes, width)

    for copy in sum_copies:
        copy.wait_recv()
    grad_sum = weight_sums[0]
    for k in range(1, replicas):
        grad_sum = grad_sum + weight_sums[k]
    unused = jnp.zeros((LANES - var_rows, LANES), F32)
    grad_out = jnp.concatenate([grad_sum, unused], axis=0).T
    columns = width // bands
    chosen = grad_out[0:columns]
    for other in range(1, ranks):
        chosen = jnp.where(rank == other, grad_out[other * columns : (other + 1) * columns], chosen)
    grad_w_out_ref[...] = chosen[:, 0:variables]

    for copy in field_copies + tile_copies + part_copies + sum_copies:
        copy.wait_send()
    for c in range(chunks):

        @pl.when(band < bands - 1)
        def _():
            halo_up[c].wait_send()
            rim_up[c].wait_send()

        @pl.when(band > 0)
        def _():
            halo_down[c].wait_send()
            rim_down[c].wait_send()


def per_device(latent, edge_weight, neighbours, band_rows, w_in, w_out, target):
    groups, bands = lax.axis_size("member"), lax.axis_size("space")
    members_dev, nodes, width = latent.shape
    rows = edge_weight.shape[1]
    variables = w_out.shape[0]
    members = groups * members_dev
    blocks = width // LANES
    replicas = groups * (bands // blocks)
    var_rows = round_up(variables, 16)
    chunks = width // STEP
    ext = round_up(3 * nodes, 256)
    vmem = pl.BlockSpec(memory_space=pltpu.VMEM)
    dma = pltpu.SemaphoreType.DMA
    score, grad_latent, grad_w_out = pl.pallas_call(
        functools.partial(kernel, (groups, bands)),
        out_shape=(
            pltpu.VMEM((1, 1), F32),
            pltpu.VMEM(latent.shape, BF16),
            pltpu.VMEM((width // bands, variables), F32),
        ),
        in_specs=[pl.BlockSpec(memory_space=pltpu.HBM)] * 7,
        out_specs=(vmem, vmem, vmem),
        scratch_shapes=[
            pltpu.VMEM(edge_weight.shape, F32),
            pltpu.VMEM(neighbours.shape, jnp.int32),
            pltpu.SMEM(band_rows.shape, jnp.int32),
            pltpu.VMEM(w_out.shape, BF16),
            pltpu.VMEM(target.shape, F32),
            pltpu.VMEM((width, width), BF16),
            pltpu.VMEM((width, width), BF16),
            pltpu.VMEM((LANES, width), BF16),
            pltpu.VMEM((width, LANES), BF16),
            pltpu.VMEM((members_dev, ext, width), BF16),
            pltpu.VMEM((rows, ext), BF16),
            pltpu.VMEM((rows, ext), BF16),
            pltpu.VMEM((2 * 3 * nodes, rows), BF16),
            pltpu.VMEM((members_dev * rows, STEP), BF16),
            pltpu.VMEM((members_dev * rows, width), BF16),
            pltpu.VMEM((members_dev * rows, width), F32),
            pltpu.VMEM((members, var_rows, rows), BF16),
            pltpu.VMEM((members, var_rows, rows), F32),
            pltpu.VMEM((var_rows, rows), F32),
            pltpu.VMEM((bands, members, LANES), F32),
            pltpu.VMEM((members, LANES), F32),
            pltpu.VMEM((members_dev, LANES, rows), F32),
            pltpu.VMEM((blocks, var_rows, LANES), BF16),
            pltpu.VMEM((blocks, var_rows, LANES), BF16),
            pltpu.VMEM((replicas, var_rows, LANES), F32),
            pltpu.VMEM((members_dev * nodes, width), F32),
            pltpu.VMEM((members_dev * nodes, width), F32),
            pltpu.VMEM((2, chunks, members_dev * nodes, STEP), BF16),
            pltpu.VMEM((2, chunks, members_dev * nodes, STEP), BF16),
            dma((7,)),
            dma((2, chunks)),
            dma((2, chunks)),
            dma((max(groups - 1, 1), members_dev)),
            dma((max(groups - 1, 1), members_dev)),
            dma((bands - 1,)),
            dma((bands - 1,)),
            dma((blocks - 1,)),
            dma((blocks - 1,)),
            dma((replicas - 1,)),
            dma((replicas - 1,)),
            dma((2, chunks)),
            dma((2, chunks)),
        ],
        compiler_params=pltpu.CompilerParams(
            collective_id=0, has_side_effects=True, vmem_limit_bytes=60 * 1024 * 1024
        ),
        name="decoder",
    )(latent, edge_weight, neighbours, band_rows, w_in, w_out, target)
    return (score[0, 0], grad_latent, grad_w_out.T)


def solution(mesh):
    return jax.shard_map(
        per_device,
        mesh=mesh,
        in_specs=(
            P("member", "space", None),
            P(None, "space"),
            P(None, "space"),
            P("space"),
            P(),
            P(),
            P(None, "space"),
        ),
        out_specs=(P(), P("member", "space", None), P(None, "space")),
        check_vma=False,
    )
```

```python
import functools

import jax
import jax.numpy as jnp
from jax import lax
from jax.experimental import pallas as pl
from jax.experimental.pallas import tpu as pltpu
from jax.sharding import PartitionSpec as P

EPSILON = 1e-06
MESH = pl.DeviceIdType.MESH
F32 = jnp.float32
BF16 = jnp.bfloat16
LANES = 128
STEP = 256


def round_up(value, unit):
    return -(-value // unit) * unit


def dot(a, b, over=((1,), (0,))):
    return lax.dot_general(a, b, (over, ((), ())), preferred_element_type=F32)


def kernel(
    sizes,
    latent_ref,
    edge_weight_hbm,
    neighbours_hbm,
    band_rows_hbm,
    w_in_hbm,
    w_out_hbm,
    target_hbm,
    score_ref,
    grad_latent_ref,
    grad_w_out_ref,
    edge_weight_ref,
    neighbours_ref,
    band_rows_ref,
    w_out_ref,
    target_ref,
    w_in,
    w_in_turned,
    w_out,
    w_out_turned,
    nodes_ext,
    spread_hi,
    spread_lo,
    collect,
    mixed,
    hidden,
    slope,
    fields_all,
    masked,
    target,
    tiles,
    coefs,
    grad_fields,
    weight_blocks,
    weight_parts,
    weight_sums,
    node_pre,
    node_own,
    rims,
    rims_in,
    load_sem,
    halo_send,
    halo_recv,
    field_send,
    field_recv,
    tile_send,
    tile_recv,
    part_send,
    part_recv,
    sum_send,
    sum_recv,
    rim_send,
    rim_recv,
):
    groups, bands = sizes
    members_dev, nodes, width = latent_ref.shape
    neigh, rows = edge_weight_ref.shape
    variables = w_out_ref.shape[0]
    members = groups * members_dev
    var_rows = fields_all.shape[1]
    blocks = width // LANES
    ranks = bands // blocks
    mine = lax.axis_index("member")
    band = lax.axis_index("space")
    block = band // ranks
    rank = lax.rem(band, ranks)

    barrier = pltpu.get_barrier_semaphore()
    partners = [(mine, lax.rem(band + k, bands)) for k in range(1, bands)]
    for k in range(1, groups):
        for other in range(ranks):
            partners.append((lax.rem(mine + k, groups), block * ranks + other))
    for partner in partners:
        pl.semaphore_signal(barrier, inc=1, device_id=partner, device_id_type=MESH)

    loads = [
        pltpu.make_async_copy(src, dst, load_sem.at[k])
        for k, (src, dst) in enumerate(
            (
                (edge_weight_hbm, edge_weight_ref),
                (neighbours_hbm, neighbours_ref),
                (latent_ref, nodes_ext.at[:, pl.ds(nodes, nodes)]),
                (band_rows_hbm, band_rows_ref),
                (target_hbm, target_ref),
                (w_out_hbm, w_out_ref),
                (w_in_hbm, w_in),
            )
        )
    ]
    for load in loads:
        load.start()
    pl.semaphore_wait(barrier, len(partners))
    chunks = width // STEP

    def remote(src, dst, send, recv, device):
        return pltpu.make_async_remote_copy(
            src_ref=src, dst_ref=dst, send_sem=send, recv_sem=recv, device_id=device, device_id_type=MESH
        )

    halo_up, halo_down = [], []
    for c in range(chunks):
        cut = pl.ds(c * STEP, STEP)
        for way, copies, low in ((0, halo_up, 0), (1, halo_down, 2 * nodes)):
            copies.append(
                remote(
                    latent_ref.at[:, :, cut],
                    nodes_ext.at[:, pl.ds(low, nodes), cut],
                    halo_send.at[way, c],
                    halo_recv.at[way, c],
                    (mine, band + 1 - 2 * way),
                )
            )
    for c in range(chunks):

        @pl.when(band < bands - 1)
        def _():
            halo_up[c].start()

        @pl.when(band > 0)
        def _():
            halo_down[c].start()

    @pl.when(band == 0)
    def _():
        nodes_ext[:, 0:nodes, :] = jnp.zeros((members_dev, nodes, width), BF16)
        rims_in[0] = jnp.zeros(rims_in.shape[1:], BF16)

    @pl.when(band == bands - 1)
    def _():
        nodes_ext[:, 2 * nodes : 3 * nodes, :] = jnp.zeros((members_dev, nodes, width), BF16)
        rims_in[1] = jnp.zeros(rims_in.shape[1:], BF16)

    ext = nodes_ext.shape[1]
    nodes_ext[:, 3 * nodes :, :] = jnp.zeros((members_dev, ext - 3 * nodes, width), BF16)
    loads[0].wait()
    loads[1].wait()
    local = neighbours_ref[...] - (band - 1) * nodes
    node_id = lax.broadcasted_iota(jnp.int32, (ext, rows), 0)
    weights = jnp.zeros((ext, rows), F32)
    for k in range(neigh):
        weights = weights + jnp.where(node_id == local[k : k + 1, :], edge_weight_ref[k : k + 1, :], 0.0)
    high = weights.astype(BF16)
    sides_rows = 3 * nodes
    collect[0:sides_rows, :] = high[0:sides_rows]
    collect[sides_rows:, :] = (weights - high.astype(F32)).astype(BF16)[0:sides_rows]
    turned = weights.T
    high = turned.astype(BF16)
    spread_hi[...] = high
    spread_lo[...] = (turned - high.astype(F32)).astype(BF16)

    for k in range(2, 6):
        loads[k].wait()
    valid = (lax.broadcasted_iota(jnp.int32, (1, rows), 1) < band_rows_ref[0]).astype(F32)
    target[...] = jnp.zeros(target.shape, F32)
    target[0:variables, :] = target_ref[...] * valid
    w_out[...] = jnp.zeros(w_out.shape, BF16)
    w_out[0:variables, :] = w_out_ref[...]
    w_out_turned[...] = w_out[...].astype(F32).T.astype(BF16)

    def at(c):
        return pl.ds(pl.multiple_of(c * STEP, STEP), STEP)

    first = mine * members_dev
    field_copies = []

    def decode(i, cut):
        of = slice(i * rows, (i + 1) * rows)

        @pl.loop(0, chunks)
        def _(n):
            preact = slope[of, at(n)] + dot(mixed[of], w_in[cut, at(n)])
            sigmoid = 0.5 + 0.5 * jnp.tanh(0.5 * preact)
            hidden[of, at(n)] = (preact * sigmoid).astype(BF16)
            slope[of, at(n)] = sigmoid * (1.0 + preact * (1.0 - sigmoid))

        decoded = dot(hidden[of, :], w_out_turned[...])
        fields_all[first + i] = decoded.T[0:var_rows].astype(BF16)
        for k in range(1, groups):
            here = fields_all.at[first + i]
            copy = remote(
                here,
                here,
                field_send.at[k - 1, i],
                field_recv.at[k - 1, i],
                (lax.rem(mine + k, groups), band),
            )
            copy.start()
            field_copies.append(copy)

    for c in range(chunks):

        @pl.when(band > 0)
        def _():
            halo_up[c].wait_recv()

        @pl.when(band < bands - 1)
        def _():
            halo_down[c].wait_recv()

        if c == 0:
            loads[6].wait()
        cut = slice(c * STEP, (c + 1) * STEP)
        for i in range(members_dev):
            of = slice(i * rows, (i + 1) * rows)
            part = nodes_ext[i, :, cut]
            mixed[of] = (dot(spread_hi[...], part) + dot(spread_lo[...], part)).astype(BF16)
            if c == chunks - 1:
                decode(i, cut)
        if c < chunks - 1:

            @pl.loop(0, chunks)
            def _(n):
                term = dot(mixed[...], w_in[cut, at(n)])
                slope[:, at(n)] = term if c == 0 else slope[:, at(n)] + term

    def turn(c):
        cut = slice(c * STEP, (c + 1) * STEP)
        w_in_turned[cut, :] = w_in[:, cut].T

    tile_shape = tiles.shape[1:]
    tile_row = lax.broadcasted_iota(jnp.int32, tile_shape, 0)
    tile_lane = lax.broadcasted_iota(jnp.int32, tile_shape, 1)

    def total(array):
        return jnp.sum(jnp.sum(array, axis=0, keepdims=True), axis=1, keepdims=True)

    def distance(a, b):
        gap = a - b
        square = gap * gap
        folded = square[:, 0:LANES]
        for k in range(1, rows // LANES):
            folded = folded + square[:, k * LANES : (k + 1) * LANES]
        return total(folded)

    tile = jnp.where(tile_lane == members + 1, total(valid), 0.0)
    if members <= 4:
        order = [lax.rem(first + k, members) for k in range(members)]
        for a in range(members):
            if a == members_dev:
                turn(0)
                for copy in field_copies:
                    copy.wait_recv()
            m = order[a]
            masked[m] = fields_all[m].astype(F32) * valid
            place = (tile_row == m) & (tile_lane == members)
            tile = jnp.where(place, distance(masked[m], target[...]), tile)
            for n in order[:a]:
                place = ((tile_row == m) & (tile_lane == n)) | ((tile_row == n) & (tile_lane == m))
                tile = jnp.where(place, distance(masked[m], masked[n]), tile)
    else:
        turn(0)
        for copy in field_copies:
            copy.wait_recv()
        for m in range(members):
            masked[m] = fields_all[m].astype(F32) * valid

        def one_member(m, tile):
            own = masked[m]
            here = tile_row == m
            tile = jnp.where(here & (tile_lane == members), distance(own, target[...]), tile)
            return lax.fori_loop(
                0,
                members,
                lambda n, t: jnp.where(here & (tile_lane == n), distance(own, masked[n]), t),
                tile,
            )

        tile = lax.fori_loop(0, members, one_member, tile)
    tiles[band] = tile
    tile_copies = []
    for k in range(1, bands):
        copy = remote(
            tiles.at[band],
            tiles.at[band],
            tile_send.at[k - 1],
            tile_recv.at[k - 1],
            (mine, lax.rem(band + k, bands)),
        )
        copy.start()
        tile_copies.append(copy)
    turn(1)
    for copy in tile_copies:
        copy.wait_recv()
    summed = tiles[0]
    for k in range(1, bands):
        summed = summed + tiles[k]

    cells = variables * summed[0:1, members + 1 : members + 2]
    dist = jnp.sqrt(summed / cells + EPSILON)
    in_rows = tile_row < members
    pair = in_rows & (tile_lane < members) & (tile_row != tile_lane)
    own_lane = in_rows & (tile_lane == members)
    score_ref[...] = total(jnp.where(own_lane, dist, 0.0)) / members - total(
        jnp.where(pair, dist, 0.0)
    ) / (2.0 * members * (members - 1))
    inverse = 1.0 / dist
    pair_coef = jnp.where(pair, inverse / (members * (members - 1)), 0.0)
    coef_sum = jnp.sum(pair_coef, axis=1, keepdims=True)
    coefs[...] = jnp.where(
        own_lane, inverse / members, jnp.where(tile_lane == members + 1, coef_sum, pair_coef)
    )
    for i in range(members_dev):
        row = coefs[pl.ds(first + i, 1), :]
        own = masked[first + i]
        others = row[:, 0:1] * masked[0]
        for n in range(1, members):
            others = others + row[:, n : n + 1] * masked[n]
        toward = (own - target[...]) * row[:, members : members + 1]
        grad = toward - (row[:, members + 1 : members + 2] * own - others)
        grad_fields[i, 0:var_rows, :] = grad
        grad_fields[i, var_rows:, :] = jnp.zeros((grad_fields.shape[1] - var_rows, rows), F32)

    part_copies = []

    def project():

        @pl.loop(0, chunks)
        def _(c):
            part = dot(grad_fields[0, 0:var_rows, :].astype(BF16), hidden[0:rows, at(c)])
            for i in range(1, members_dev):
                part = part + dot(
                    grad_fields[i, 0:var_rows, :].astype(BF16), hidden[i * rows : (i + 1) * rows, at(c)]
                )
            for j in range(STEP // LANES):
                weight_blocks[c * (STEP // LANES) + j] = part[:, j * LANES : (j + 1) * LANES].astype(BF16)

        for k in range(1, blocks):
            there = lax.rem(block + k, blocks)
            copy = remote(
                weight_blocks.at[there],
                weight_parts.at[block],
                part_send.at[k - 1],
                part_recv.at[k - 1],
                (mine, there * ranks + rank),
            )
            copy.start()
            part_copies.append(copy)
        weight_parts[block] = weight_blocks[block]

    side_rows = members_dev * nodes
    turned_grads = [grad_fields[i].T.astype(BF16) for i in range(members_dev)]
    rim_down, rim_up = [], []
    for c in range(chunks):
        cut = slice(c * STEP, (c + 1) * STEP)
        for i in range(members_dev):
            back = dot(turned_grads[i], w_out[:, cut])
            grad_pre = (back * slope[i * rows : (i + 1) * rows, cut]).astype(BF16)
            terms = dot(collect[...], grad_pre)
            gathered = terms[0:sides_rows] + terms[sides_rows:]
            of = slice(i * nodes, (i + 1) * nodes)
            rims[0, c, of] = gathered[0:nodes].astype(BF16)
            node_pre[of, cut] = gathered[nodes : 2 * nodes]
            rims[1, c, of] = gathered[2 * nodes :].astype(BF16)
        rim_down.append(
            remote(rims.at[0, c], rims_in.at[1, c], rim_send.at[0, c], rim_recv.at[0, c], (mine, band - 1))
        )
        rim_up.append(
            remote(rims.at[1, c], rims_in.at[0, c], rim_send.at[1, c], rim_recv.at[1, c], (mine, band + 1))
        )

        @pl.when(band > 0)
        def _():
            rim_down[c].start()

        @pl.when(band < bands - 1)
        def _():
            rim_up[c].start()

        if c == 0:
            project()

    replicas = groups * ranks
    sum_copies = []

    def share():
        for copy in part_copies:
            copy.wait_recv()
        part = weight_parts[0].astype(F32)
        for j in range(1, blocks):
            part = part + weight_parts[j].astype(F32)
        replica = mine * ranks + rank
        weight_sums[replica] = part
        for k in range(1, replicas):
            there = lax.rem(replica + k, replicas)
            copy = remote(
                weight_sums.at[replica],
                weight_sums.at[replica],
                sum_send.at[k - 1],
                sum_recv.at[k - 1],
                (there // ranks, block * ranks + lax.rem(there, ranks)),
            )
            copy.start()
            sum_copies.append(copy)

    for c in range(2, chunks):
        turn(c)
    for c in range(chunks):

        @pl.when(band < bands - 1)
        def _():
            rim_down[c].wait_recv()

        @pl.when(band > 0)
        def _():
            rim_up[c].wait_recv()

        cut = slice(c * STEP, (c + 1) * STEP)
        node_sum = node_pre[:, cut] + rims_in[1, c].astype(F32) + rims_in[0, c].astype(F32)
        term = dot(node_sum.astype(BF16), w_in_turned[cut, :])
        node_own[...] = term if c == 0 else node_own[...] + term
        if c == chunks // 2:
            share()

    grad_latent_ref[...] = node_own[...].astype(BF16).reshape(members_dev, nodes, width)

    for copy in sum_copies:
        copy.wait_recv()
    grad_sum = weight_sums[0]
    for k in range(1, replicas):
        grad_sum = grad_sum + weight_sums[k]
    unused = jnp.zeros((LANES - var_rows, LANES), F32)
    grad_out = jnp.concatenate([grad_sum, unused], axis=0).T
    columns = width // bands
    chosen = grad_out[0:columns]
    for other in range(1, ranks):
        chosen = jnp.where(rank == other, grad_out[other * columns : (other + 1) * columns], chosen)
    grad_w_out_ref[...] = chosen[:, 0:variables]

    for copy in field_copies + tile_copies + part_copies + sum_copies:
        copy.wait_send()
    for c in range(chunks):

        @pl.when(band < bands - 1)
        def _():
            halo_up[c].wait_send()
            rim_up[c].wait_send()

        @pl.when(band > 0)
        def _():
            halo_down[c].wait_send()
            rim_down[c].wait_send()


def per_device(latent, edge_weight, neighbours, band_rows, w_in, w_out, target):
    groups, bands = lax.axis_size("member"), lax.axis_size("space")
    members_dev, nodes, width = latent.shape
    rows = edge_weight.shape[1]
    variables = w_out.shape[0]
    members = groups * members_dev
    blocks = width // LANES
    replicas = groups * (bands // blocks)
    var_rows = round_up(variables, 16)
    chunks = width // STEP
    ext = round_up(3 * nodes, 256)
    vmem = pl.BlockSpec(memory_space=pltpu.VMEM)
    dma = pltpu.SemaphoreType.DMA
    score, grad_latent, grad_w_out = pl.pallas_call(
        functools.partial(kernel, (groups, bands)),
        out_shape=(
            pltpu.VMEM((1, 1), F32),
            pltpu.VMEM(latent.shape, BF16),
            pltpu.VMEM((width // bands, variables), F32),
        ),
        in_specs=[pl.BlockSpec(memory_space=pltpu.HBM)] * 7,
        out_specs=(vmem, vmem, vmem),
        scratch_shapes=[
            pltpu.VMEM(edge_weight.shape, F32),
            pltpu.VMEM(neighbours.shape, jnp.int32),
            pltpu.SMEM(band_rows.shape, jnp.int32),
            pltpu.VMEM(w_out.shape, BF16),
            pltpu.VMEM(target.shape, F32),
            pltpu.VMEM((width, width), BF16),
            pltpu.VMEM((width, width), BF16),
            pltpu.VMEM((LANES, width), BF16),
            pltpu.VMEM((width, LANES), BF16),
            pltpu.VMEM((members_dev, ext, width), BF16),
            pltpu.VMEM((rows, ext), BF16),
            pltpu.VMEM((rows, ext), BF16),
            pltpu.VMEM((2 * 3 * nodes, rows), BF16),
            pltpu.VMEM((members_dev * rows, STEP), BF16),
            pltpu.VMEM((members_dev * rows, width), BF16),
            pltpu.VMEM((members_dev * rows, width), F32),
            pltpu.VMEM((members, var_rows, rows), BF16),
            pltpu.VMEM((members, var_rows, rows), F32),
            pltpu.VMEM((var_rows, rows), F32),
            pltpu.VMEM((bands, members, LANES), F32),
            pltpu.VMEM((members, LANES), F32),
            pltpu.VMEM((members_dev, LANES, rows), F32),
            pltpu.VMEM((blocks, var_rows, LANES), BF16),
            pltpu.VMEM((blocks, var_rows, LANES), BF16),
            pltpu.VMEM((replicas, var_rows, LANES), F32),
            pltpu.VMEM((members_dev * nodes, width), F32),
            pltpu.VMEM((members_dev * nodes, width), F32),
            pltpu.VMEM((2, chunks, members_dev * nodes, STEP), BF16),
            pltpu.VMEM((2, chunks, members_dev * nodes, STEP), BF16),
            dma((7,)),
            dma((2, chunks)),
            dma((2, chunks)),
            dma((max(groups - 1, 1), members_dev)),
            dma((max(groups - 1, 1), members_dev)),
            dma((bands - 1,)),
            dma((bands - 1,)),
            dma((blocks - 1,)),
            dma((blocks - 1,)),
            dma((replicas - 1,)),
            dma((replicas - 1,)),
            dma((2, chunks)),
            dma((2, chunks)),
        ],
        compiler_params=pltpu.CompilerParams(
            collective_id=0, has_side_effects=True, vmem_limit_bytes=60 * 1024 * 1024
        ),
        name="decoder",
    )(latent, edge_weight, neighbours, band_rows, w_in, w_out, target)
    return (score[0, 0], grad_latent, grad_w_out.T)


def solution(mesh):
    return jax.shard_map(
        per_device,
        mesh=mesh,
        in_specs=(
            P("member", "space", None),
            P(None, "space"),
            P(None, "space"),
            P("space"),
            P(),
            P(),
            P(None, "space"),
        ),
        out_specs=(P(), P("member", "space", None), P(None, "space")),
        check_vma=False,
    )
```
